512 devices in a mesh: section: 4 (over z_lo), dp: 16 (over z_hi, y), mp: 8 (over x, core).
Axes of the slice: x: 4, y: 4, z: 16 (z_hi: 4, z_lo: 4; z = z_hi * 4 + z_lo), core: 2. Of those that a mesh axis runs over, the one named last changes fastest.
Arguments:
- activations: bfloat16 [4, 80, 14, 14, 4096], P('section', 'dp', None, None, 'mp'), may hold values from -180 to 180
- conv_weight: bfloat16 [4, 4096, 2048], P('section', None, 'mp'), may hold values from -0.09375 to 0.09375
- norm_gain: float32 [4, 2048], P('section', 'mp'), may hold values from 0.5 to 2
- norm_bias: float32 [4, 2048], P('section', 'mp'), may hold values from -3 to 3
- cotangent: bfloat16 [4, 80, 7, 7, 2048], P('section', 'dp', None, None, 'mp'), may hold values from -60 to 60
Outputs:
- block_out: bfloat16 [4, 80, 7, 7, 2048], P('section', 'dp', None, None, 'mp')
- grad_input: bfloat16 [4, 80, 7, 7, 4096], P('section', 'dp', None, None, 'mp')
- grad_weight: bfloat16 [4, 4096, 2048], P('section', 'dp', 'mp')
- grad_gain: float32 [4, 2048], P('section', 'mp')
- grad_bias: float32 [4, 2048], P('section', 'mp')
The draws below stay inside these ranges and needn't reach their ends.
All inputs are finite; a program needn't handle non-finite values.
Results may differ from the reference program's by a relative error of at most 0.023.
Values may be sent and summed in bfloat16 or wider, within the bound.
A program may use at most 64 MiB of HBM per device.

```python
import math
import jax
import jax.numpy as jnp
from jax import lax

CIN = 4096
MID = 2048
H = 14
H2 = 7
BATCH = 80
SECTIONS = 4
N_DP = 16
N_MP = 8


def draw_activations(key, part):
    key = jax.random.fold_in(key, 11)
    key_base, key_pixel, key_chan = jax.random.split(key, 3)
    shape = (SECTIONS, BATCH, H, H, CIN)
    base = jnp.clip(jax.random.normal(key_base, shape, jnp.float32), -6.0, 6.0)
    chan_scale = jnp.exp(jax.random.uniform(key_chan, (CIN,), jnp.float32, 0.0, math.log(10.0)))
    pixel_scale = jnp.exp(jax.random.uniform(key_pixel, (SECTIONS, BATCH, H, H, 1), jnp.float32, 0.0, math.log(10.0)))
    ramp = jnp.exp(math.log(3.0) * jnp.arange(BATCH, dtype=jnp.float32) / max(BATCH - 1, 1)).reshape(1, BATCH, 1, 1, 1)
    return (base * pixel_scale * chan_scale * ramp / 10.0).astype(jnp.bfloat16)


def draw_cotangent(key, part):
    key = jax.random.fold_in(key, 23)
    key_base, key_pixel = jax.random.split(key, 2)
    shape = (SECTIONS, BATCH, H2, H2, MID)
    base = jnp.clip(jax.random.normal(key_base, shape, jnp.float32), -6.0, 6.0)
    pixel_scale = jnp.exp(jax.random.uniform(key_pixel, (SECTIONS, BATCH, H2, H2, 1), jnp.float32, 0.0, math.log(10.0)))
    ramp = jnp.exp(math.log(3.0) * jnp.arange(BATCH, dtype=jnp.float32) / max(BATCH - 1, 1)).reshape(1, BATCH, 1, 1, 1)
    return (base * pixel_scale * ramp / 3.0).astype(jnp.bfloat16)


def block_scale(rng, shape, cuts, low, high):
    level, own = 1.0, jax.random.fold_in(rng, 6)
    for axis_at, blocks in cuts:
        heights = jnp.exp(jax.random.uniform(jax.random.fold_in(own, axis_at), (blocks,), jnp.float32, low / len(cuts), high / len(cuts)))
        level = level * jnp.repeat(heights, shape[axis_at] // blocks).reshape([-1 if axis == axis_at else 1 for axis in range(len(shape))])
    return level


def bell_draw(own_key, dims, deviation, most, shards=(), kind=jnp.bfloat16):
    drawn = deviation * jax.random.normal(own_key, dims, jnp.float32)
    if shards:
        drawn = drawn * block_scale(own_key, dims, shards, -0.22, 0.18)
    return jnp.clip(drawn, -most, most).astype(kind)


def setup_inputs(seed: int = 0) -> dict:
    seeds = jax.random.split(jax.random.key(seed), 6)
    activations = draw_activations(jax.random.fold_in(seeds[5], 71), 0)
    conv_weight = bell_draw(seeds[1], (SECTIONS, CIN, MID), CIN ** -0.5, 0.09375, ((0, 4), (2, 8)))
    norm_gain = jnp.clip(jnp.exp(math.log(2.0) - 1.3862944 * jax.random.uniform(seeds[2], (SECTIONS, MID), jnp.float32) ** block_scale(seeds[2], (SECTIONS, MID), ((0, 4), (1, 8)), -0.2, 0.2)), 0.5, 2.0)
    norm_bias = bell_draw(seeds[3], (SECTIONS, MID), 0.5, 3.0, ((0, 4), (1, 8)), jnp.float32)
    cotangent = draw_cotangent(jax.random.fold_in(seeds[5], 71), 0)
    return {"activations": activations, "conv_weight": conv_weight, "norm_gain": norm_gain, "norm_bias": norm_bias, "cotangent": cotangent}


def section_block(sampled, weight, gain, bias, grad_out):
    total_rows = sampled.shape[0]
    hidden = jnp.dot(sampled, weight, preferred_element_type=jnp.float32)
    average = lax.optimization_barrier(jnp.sum(hidden, axis=0)) / total_rows
    centred = hidden - average
    spread = lax.optimization_barrier(jnp.sum(centred * centred, axis=0)) / total_rows
    inverse = lax.rsqrt(spread + 1e-05)
    normed = centred * inverse
    pre_act = gain * normed + bias
    squash = jax.nn.sigmoid(pre_act)
    block_out = (pre_act * squash).astype(jnp.bfloat16)
    grad_pre = grad_out.astype(jnp.float32) * squash * (1.0 + pre_act * (1.0 - squash))
    bias_grad = lax.optimization_barrier(jnp.sum(grad_pre, axis=0))
    gain_grad = lax.optimization_barrier(jnp.sum(grad_pre * normed, axis=0))
    grad_hidden = (gain * inverse * (grad_pre - bias_grad / total_rows - normed * (gain_grad / total_rows))).astype(jnp.bfloat16)
    group_rows = total_rows // N_DP
    weight_sum = jnp.zeros((CIN, MID), jnp.float32)
    for member in range(N_DP):
        rows_part = sampled[member * group_rows:(member + 1) * group_rows]
        grad_part = grad_hidden[member * group_rows:(member + 1) * group_rows]
        partial_value = jnp.dot(rows_part.T, grad_part, preferred_element_type=jnp.float32).astype(jnp.bfloat16)
        partial_value = lax.optimization_barrier(partial_value)
        weight_sum = weight_sum + partial_value.astype(jnp.float32)
    group_cols = MID // N_MP
    input_sum = jnp.zeros((total_rows, CIN), jnp.float32)
    for member in range(N_MP):
        grad_part = grad_hidden[:, member * group_cols:(member + 1) * group_cols]
        weight_part = weight[:, member * group_cols:(member + 1) * group_cols]
        partial_value = jnp.dot(grad_part, weight_part.T, preferred_element_type=jnp.float32).astype(jnp.bfloat16)
        partial_value = lax.optimization_barrier(partial_value)
        input_sum = input_sum + partial_value.astype(jnp.float32)
    return (block_out, input_sum.astype(jnp.bfloat16), weight_sum.astype(jnp.bfloat16), gain_grad, bias_grad)

def reference(activations, conv_weight, norm_gain, norm_bias, cotangent):
    outs_list = [None] * SECTIONS
    inputs_list = [None] * SECTIONS
    weights_list = [None] * SECTIONS
    gains_list = [None] * SECTIONS
    biases_list = [None] * SECTIONS
    for current in range(SECTIONS):
        partner = current ^ 1
        sampled = activations[partner][:, ::2, ::2, :].reshape(BATCH * H2 * H2, CIN)
        grad_out = cotangent[current].reshape(BATCH * H2 * H2, MID)
        block_out, input_grad, weight_grad, gain_grad, bias_grad = section_block(sampled, conv_weight[current], norm_gain[current], norm_bias[current], grad_out)
        outs_list[current] = block_out.reshape(BATCH, H2, H2, MID)
        inputs_list[partner] = input_grad.reshape(BATCH, H2, H2, CIN)
        weights_list[current] = weight_grad
        gains_list[current] = gain_grad
        biases_list[current] = bias_grad
    return (jnp.stack(outs_list), jnp.stack(inputs_list), jnp.stack(weights_list), jnp.stack(gains_list), jnp.stack(biases_list))
```

```python
import functools

import jax
import jax.numpy as jnp
from jax import lax
from jax.experimental import pallas as pl
from jax.experimental.pallas import tpu as pltpu
from jax.sharding import PartitionSpec as P

BF16 = jnp.bfloat16
F32 = jnp.float32
RING = 4
ROWS = 245
PAD = 256
HALF = PAD // 2
CH = 512
COLS = 256
TILE = 16
STRIPS = 35
COPIES = 64


def dot(a, b, over):
    return lax.dot_general(a, b, ((over[:1], over[1:]), ((), ())), preferred_element_type=F32)


def picks(step):
    shape = (PAD, STRIPS * TILE)
    row = lax.broadcasted_iota(jnp.int32, shape, 0)
    col = lax.broadcasted_iota(jnp.int32, shape, 1)
    pixel = col & (TILE - 1)
    wanted = 7 * (col >> 4) + (pixel if step == 1 else pixel >> 1)
    keep = (row == wanted) & (pixel < 7 * step)
    if step == 2:
        keep = keep & ((pixel & 1) == 0)
    return jnp.where(keep, 1.0, 0.0).astype(F32).astype(BF16)


def kernel(
    acts, weight, gain_ref, shift_ref, cotan,
    block_out, grad_input, grad_weight, gain_grad, bias_grad,
    raw, strips, w, ct_raw, ct_strips, own, full, ex, gh, hid,
    ys, zs, yg, zg,
    to_sib, from_sib, xb, x_opp, x_left, x_right,
    zb, z_opp, z_left, z_right, share, returned,
    send_sems, recv_sems, local_sems,
):
    section, dp, mp = lax.axis_index("section"), lax.axis_index("dp"), lax.axis_index("mp")
    zh, y = lax.div(dp, RING), lax.rem(dp, RING)
    x, core = lax.div(mp, 2), lax.rem(mp, 2)

    def around(at, by):
        return lax.rem(at + by, RING)

    partner = {"section": section + 1 - 2 * lax.rem(section, 2)}
    sibling = {"mp": 2 * x + 1 - core}
    at_x = [{"mp": 2 * around(x, o) + core} for o in range(RING)]
    at_y = [{"dp": RING * zh + around(y, o)} for o in range(RING)]
    at_z = [{"dp": RING * around(zh, o) + y} for o in range(RING)]
    peers = [partner, sibling, at_x[1], at_x[3]] + at_y[1:] + at_z[1:]

    started = []
    ids = iter(range(COPIES))

    def names(n):
        return [next(ids) for _ in range(n)]

    def send(src, dst, k, to):
        copy = pltpu.make_async_remote_copy(
            src_ref=src, dst_ref=dst, send_sem=send_sems.at[k], recv_sem=recv_sems.at[k],
            device_id=to, device_id_type=pl.DeviceIdType.MESH,
        )
        copy.start()
        started.append(copy)

    def arrive(dst, k):
        pltpu.make_async_remote_copy(
            src_ref=dst, dst_ref=dst, send_sem=send_sems.at[k], recv_sem=recv_sems.at[k],
            device_id=sibling, device_id_type=pl.DeviceIdType.MESH,
        ).wait_recv()

    load_acts = pltpu.make_async_copy(acts.at[:, :, 0], raw, local_sems.at[0])
    load_w = pltpu.make_async_copy(weight, w, local_sems.at[1])
    load_ct = pltpu.make_async_copy(cotan, ct_raw, local_sems.at[2])
    load_acts.start()
    load_w.start()
    load_ct.start()
    barrier = pltpu.get_barrier_semaphore()
    for peer in peers:
        pl.semaphore_signal(barrier, inc=1, device_id=peer, device_id_type=pl.DeviceIdType.MESH)
    strips[...] = jnp.zeros_like(strips)
    ct_strips[...] = jnp.zeros_like(ct_strips)
    load_acts.wait()
    strips[:, 0:14, :] = raw[...].reshape(STRIPS, 14, CH)
    own[...] = dot(picks(2), strips[...].reshape(STRIPS * TILE, CH), (1, 0)).astype(BF16)
    pl.semaphore_wait(barrier, len(peers))

    halves = [pl.ds(0, HALF), pl.ds(HALF, HALF)]
    k_part, k_left, k_right, k_sib = names(2), names(2), names(2), names(2)
    k_sl, k_sr, k_so, k_opp = names(2), names(2), names(2), names(2)
    for h in range(2):
        send(own.at[halves[h]], full.at[x, core, halves[h]], k_part[h], partner)
    for h in range(2):
        mine = full.at[x, core, halves[h]]
        arrive(mine, k_part[h])
        send(mine, mine, k_right[h], at_x[1])
        send(mine, mine, k_left[h], at_x[3])
        send(mine, mine, k_sib[h], sibling)
    load_ct.wait()
    ct_strips[:, 0:7, :] = ct_raw[...].reshape(STRIPS, 7, COLS)
    grad_out = dot(picks(1), ct_strips[...].reshape(STRIPS * TILE, COLS), (1, 0))
    load_w.wait()

    def w_block(xx, cc):
        return w[pl.ds(pl.multiple_of(CH * (2 * xx + cc), CH), CH), :]

    def term(xx, cc):
        return dot(full[xx, cc], w_block(xx, cc), (1, 0))

    lx, rx, ox = around(x, 3), around(x, 1), around(x, 2)
    for h in range(2):
        from_left = full.at[lx, core, halves[h]]
        arrive(from_left, k_right[h])
        if h == 0:
            send(from_left, from_left, k_opp[0], at_x[1])
        send(from_left, from_left, k_sl[h], sibling)
        from_right = full.at[rx, core, halves[h]]
        arrive(from_right, k_left[h])
        if h == 1:
            send(from_right, from_right, k_opp[1], at_x[3])
        send(from_right, from_right, k_sr[h], sibling)
    hid[...] = term(x, core)
    for h in range(2):
        arrive(full.at[x, 1 - core, halves[h]], k_sib[h])
    hid[...] += term(x, 1 - core)
    hid[...] += term(lx, core)
    hid[...] += term(rx, core)
    for h in range(2):
        arrive(full.at[lx, 1 - core, halves[h]], k_sl[h])
    hid[...] += term(lx, 1 - core)
    for h in range(2):
        arrive(full.at[rx, 1 - core, halves[h]], k_sr[h])
    hid[...] += term(rx, 1 - core)
    for h in range(2):
        opposite = full.at[ox, core, halves[h]]
        arrive(opposite, k_opp[h])
        send(opposite, opposite, k_so[h], sibling)
    hid[...] += term(ox, core)
    for h in range(2):
        arrive(full.at[ox, 1 - core, halves[h]], k_so[h])
    hid[...] += term(ox, 1 - core)
    hidden = hid[...]

    def spread_out(buf, me, to, value, ks):
        buf[me] = value
        for o in range(1, RING):
            send(buf.at[me], buf.at[me], ks[o - 1], to[o])

    def collect(buf, me, ks):
        for o in range(1, RING):
            arrive(buf.at[around(me, RING - o)], ks[o - 1])

    def two_rows(a, b):
        row = lax.broadcasted_iota(jnp.int32, (8, COLS), 0)
        return jnp.where(row == 0, a, jnp.where(row == 1, b, 0.0))

    def merge(buf, count):
        means = [buf[i, 0:1, :] for i in range(RING)]
        squares = [buf[i, 1:2, :] for i in range(RING)]
        mean = sum(means) / RING
        return mean, sum(squares) + count * sum((m - mean) * (m - mean) for m in means)

    valid = lax.broadcasted_iota(jnp.int32, (PAD, COLS), 0) < ROWS
    mean = jnp.sum(hidden, axis=0, keepdims=True) / ROWS
    off = jnp.where(valid, hidden - mean, 0.0)
    square = jnp.sum(off * off, axis=0, keepdims=True)
    k_ys, k_zs, k_yg, k_zg = names(3), names(3), names(3), names(3)
    spread_out(ys, y, at_y, two_rows(mean, square), k_ys)

    k_ex, k_es = names(3), names(3)

    def quarter(yy, rows):
        at = pl.multiple_of(COLS * lax.rem(yy, 2), COLS)
        return full.at[:, lax.div(yy, 2), rows, pl.ds(at, COLS)]

    def ex_rows(yy, cc):
        return ex.at[:, pl.ds(pl.multiple_of(PAD * yy + HALF * cc, HALF), HALF), :]

    my_rows = pl.ds(pl.multiple_of(HALF * core, HALF), HALF)
    for o in (2, 1, 3):
        send(quarter(around(y, o), my_rows), ex_rows(y, core), k_ex[o - 1], at_y[o])
    keep = pltpu.make_async_copy(
        quarter(y, pl.ds(0, PAD)),
        ex.at[:, pl.ds(pl.multiple_of(PAD * y, PAD), PAD), :],
        local_sems.at[3],
    )
    keep.start()

    collect(ys, y, k_ys)
    mean, square = merge(ys, float(ROWS))
    spread_out(zs, zh, at_z, two_rows(mean, square), k_zs)
    collect(zs, zh, k_zs)
    mean, square = merge(zs, float(ROWS * RING))
    total = float(ROWS * RING * RING)
    inverse = lax.rsqrt(square / total + 1e-05)
    gain, shift = gain_ref[...], shift_ref[...]
    normed = (hidden - mean) * inverse
    pre_act = gain * normed + shift
    squash = jax.nn.sigmoid(pre_act)
    grad_pre = grad_out * squash * (1.0 + pre_act * (1.0 - squash))
    d_bias = jnp.sum(grad_pre, axis=0, keepdims=True)
    d_gain = jnp.sum(grad_pre * normed, axis=0, keepdims=True)
    spread_out(yg, y, at_y, two_rows(d_bias, d_gain), k_yg)
    spaced = dot(picks(1), (pre_act * squash).astype(BF16), (0, 0)).reshape(STRIPS, TILE, COLS)
    block_out[...] = spaced[:, 0:7, :].astype(BF16)
    collect(yg, y, k_yg)
    spread_out(zg, zh, at_z, yg[0] + yg[1] + yg[2] + yg[3], k_zg)
    collect(zg, zh, k_zg)
    sums = zg[0] + zg[1] + zg[2] + zg[3]
    d_bias, d_gain = sums[0:1, :], sums[1:2, :]
    bias_grad[...] = d_bias
    gain_grad[...] = d_gain
    grad_hidden = (
        gain * inverse * (grad_pre - d_bias / total - normed * (d_gain / total))
    ).astype(BF16)

    k_up, k_down, k_far = names(2), names(2), names(2)

    def gh_rows(yy, h):
        return gh.at[pl.ds(pl.multiple_of(PAD * yy + HALF * h, HALF), HALF), :]

    gh[pl.ds(pl.multiple_of(PAD * y, PAD), PAD), :] = grad_hidden
    for h in range(2):
        send(gh_rows(y, h), gh_rows(y, h), k_up[h], at_y[1])
        send(gh_rows(y, h), gh_rows(y, h), k_down[h], at_y[3])

    k_cs = names(4)
    order = (2, 1, 3, 0)
    for o in order:
        to_sib[o] = dot(grad_hidden, w_block(around(x, o), 1 - core), (1, 1)).astype(BF16)
        send(to_sib.at[o], from_sib.at[o], k_cs[o], sibling)

    for o in (1, 3, 2):
        yy = around(y, RING - o)
        arrive(ex_rows(yy, core), k_ex[o - 1])
        send(ex_rows(yy, core), ex_rows(yy, core), k_es[o - 1], sibling)

    ly, ry, oy = around(y, 3), around(y, 1), around(y, 2)
    arrive(gh_rows(ly, 0), k_up[0])
    send(gh_rows(ly, 0), gh_rows(ly, 0), k_far[0], at_y[1])
    arrive(gh_rows(ry, 0), k_down[0])
    arrive(gh_rows(ry, 1), k_down[1])
    send(gh_rows(ry, 1), gh_rows(ry, 1), k_far[1], at_y[3])
    arrive(gh_rows(ly, 1), k_up[1])

    def ring_start(block, opp, left, right, to, ks):
        send(block.at[2, halves[0]], opp.at[0], ks[0], to[1])
        send(block.at[2, halves[1]], opp.at[1], ks[1], to[3])
        send(block.at[1, halves[1]], left.at[1], ks[2], to[1])
        send(block.at[3, halves[0]], right.at[0], ks[3], to[3])

    def ring_middle(block, opp, left, right, to, ks):
        arrive(opp.at[0], ks[0])
        block[1, halves[0]] = (block[1, halves[0]].astype(F32) + opp[0].astype(F32)).astype(BF16)
        send(block.at[1, halves[0]], left.at[0], ks[4], to[1])
        arrive(opp.at[1], ks[1])
        block[3, halves[1]] = (block[3, halves[1]].astype(F32) + opp[1].astype(F32)).astype(BF16)
        send(block.at[3, halves[1]], right.at[1], ks[5], to[3])

    def ring_end(block, left, right, ks):
        arrive(left.at[1], ks[2])
        arrive(right.at[0], ks[3])
        arrive(left.at[0], ks[4])
        arrive(right.at[1], ks[5])
        out = []
        for h in range(2):
            out.append(
                block[0, halves[h]].astype(F32) + left[h].astype(F32) + right[h].astype(F32)
            )
        return [part.astype(BF16) for part in out]

    k_x, k_z, k_back = names(6), names(6), names(1)
    for o in order:
        part = dot(grad_hidden, w_block(around(x, o), core), (1, 1))
        arrive(from_sib.at[o], k_cs[o])
        xb[o] = (part + from_sib[o].astype(F32)).astype(BF16)
    ring_start(xb, x_opp, x_left, x_right, at_x, k_x)

    arrive(gh_rows(oy, 0), k_far[0])
    arrive(gh_rows(oy, 1), k_far[1])
    keep.wait()
    for o in (1, 3, 2):
        yy = around(y, RING - o)
        arrive(ex_rows(yy, 1 - core), k_es[o - 1])
    for o in order:
        zb[o] = dot(ex[around(zh, o)], gh[...], (0, 0)).astype(BF16)
    ring_start(zb, z_opp, z_left, z_right, at_z, k_z)

    ring_middle(xb, x_opp, x_left, x_right, at_x, k_x)
    halves_x = ring_end(xb, x_left, x_right, k_x)
    for h in range(2):
        share[halves[h], :] = halves_x[h]
    send(share, returned, k_back[0], partner)

    ring_middle(zb, z_opp, z_left, z_right, at_z, k_z)
    arrive(returned, k_back[0])
    spaced = dot(picks(1), returned[...], (0, 0)).reshape(STRIPS, TILE, CH)
    grad_input[...] = spaced[:, 0:7, :].astype(BF16)

    halves_z = ring_end(zb, z_left, z_right, k_z)
    for h in range(2):
        grad_weight[halves[h], :] = halves_z[h]
    for copy in started:
        copy.wait_send()


def on_device(activations, conv_weight, norm_gain, norm_bias, cotangent):
    images = activations.shape[1]
    acts = activations.reshape(images, 7, 2, 14, CH)
    cotan = cotangent.reshape(images, 7, 7, COLS)
    hbm = pl.BlockSpec(memory_space=pl.ANY)
    vmem = pl.BlockSpec(memory_space=pltpu.VMEM)
    block_out, grad_input, grad_weight, gain_grad, bias_grad = pl.pallas_call(
        kernel,
        out_shape=(
            jax.ShapeDtypeStruct((STRIPS, 7, COLS), BF16),
            jax.ShapeDtypeStruct((STRIPS, 7, CH), BF16),
            jax.ShapeDtypeStruct((COLS, COLS), BF16),
            jax.ShapeDtypeStruct((1, COLS), F32),
            jax.ShapeDtypeStruct((1, COLS), F32),
        ),
        in_specs=[hbm, hbm, vmem, vmem, hbm],
        out_specs=[vmem] * 5,
        scratch_shapes=[
            pltpu.VMEM((images, 7, 14, CH), BF16),
            pltpu.VMEM((STRIPS, TILE, CH), BF16),
            pltpu.VMEM((RING * 2 * CH, COLS), BF16),
            pltpu.VMEM((images, 7, 7, COLS), BF16),
            pltpu.VMEM((STRIPS, TILE, COLS), BF16),
            pltpu.VMEM((PAD, CH), BF16),
            pltpu.VMEM((RING, 2, PAD, CH), BF16),
            pltpu.VMEM((RING, RING * PAD, COLS), BF16),
            pltpu.VMEM((RING * PAD, COLS), BF16),
            pltpu.VMEM((PAD, COLS), F32),
            pltpu.VMEM((RING, 8, COLS), F32),
            pltpu.VMEM((RING, 8, COLS), F32),
            pltpu.VMEM((RING, 8, COLS), F32),
            pltpu.VMEM((RING, 8, COLS), F32),
            pltpu.VMEM((RING, PAD, CH), BF16),
            pltpu.VMEM((RING, PAD, CH), BF16),
            pltpu.VMEM((RING, PAD, CH), BF16),
            pltpu.VMEM((2, HALF, CH), BF16),
            pltpu.VMEM((2, HALF, CH), BF16),
            pltpu.VMEM((2, HALF, CH), BF16),
            pltpu.VMEM((RING, PAD, COLS), BF16),
            pltpu.VMEM((2, HALF, COLS), BF16),
            pltpu.VMEM((2, HALF, COLS), BF16),
            pltpu.VMEM((2, HALF, COLS), BF16),
            pltpu.VMEM((PAD, CH), BF16),
            pltpu.VMEM((PAD, CH), BF16),
            pltpu.SemaphoreType.DMA((COPIES,)),
            pltpu.SemaphoreType.DMA((COPIES,)),
            pltpu.SemaphoreType.DMA((4,)),
        ],
        compiler_params=pltpu.CompilerParams(
            collective_id=0, has_side_effects=True, vmem_limit_bytes=48 * 2**20
        ),
        name="bottleneck",
    )(acts, conv_weight[0], norm_gain, norm_bias, cotan)
    return (
        block_out.reshape(1, images, 7, 7, COLS),
        grad_input.reshape(1, images, 7, 7, CH),
        grad_weight[None],
        gain_grad,
        bias_grad,
    )


def solution(mesh):
    placed = (
        P("section", "dp", None, None, "mp"),
        P("section", None, "mp"),
        P("section", "mp"),
        P("section", "mp"),
        P("section", "dp", None, None, "mp"),
    )
    return jax.shard_map(
        on_device,
        mesh=mesh,
        in_specs=placed,
        out_specs=(
            P("section", "dp", None, None, "mp"),
            P("section", "dp", None, None, "mp"),
            P("section", "dp", "mp"),
            P("section", "mp"),
            P("section", "mp"),
        ),
        check_vma=False,
    )
```

```python
import functools

import jax
import jax.numpy as jnp
from jax import lax
from jax.experimental import pallas as pl
from jax.experimental.pallas import tpu as pltpu
from jax.sharding import PartitionSpec as P

BF16 = jnp.bfloat16
F32 = jnp.float32
RING = 4
ROWS = 245
PAD = 256
HALF = PAD // 2
CH = 512
COLS = 256
TILE = 16
STRIPS = 35
COPIES = 144
FAR_FIRST = (8, 7, 9, 6, 10, 5, 11, 4, 12, 3, 13, 2, 14, 1, 15)
BAND = 64
PARTS = 4
VMEM_BYTES = 40 * 2**20


def dot(a, b, over):
    return lax.dot_general(a, b, ((over[:1], over[1:]), ((), ())), preferred_element_type=F32)


def picks(step, back=False):
    shape = (STRIPS * TILE, PAD) if back else (PAD, STRIPS * TILE)
    row = lax.broadcasted_iota(jnp.int32, shape, 1 if back else 0)
    col = lax.broadcasted_iota(jnp.int32, shape, 0 if back else 1)
    pixel = col & (TILE - 1)
    wanted = 7 * (col >> 4) + (pixel if step == 1 else pixel >> 1)
    keep = (row == wanted) & (pixel < 7 * step)
    if step == 2:
        keep = keep & ((pixel & 1) == 0)
    return jnp.where(keep, 1.0, 0.0).astype(F32).astype(BF16)


def kernel(
    acts, weight, gain_hbm, shift_hbm, cotan,
    block_out, grad_input, grad_weight, gain_grad, bias_grad,
    raw, strips, w, gain_ref, shift_ref, ct_raw, ct_strips, pick, own, full, ex, mine, gh, hid, cot, acted,
    stat, grad,
    to_sib, from_sib, xb, x_opp, x_left, x_right,
    zb, z_opp, z_left, z_right, share, returned,
    send_sems, recv_sems, local_sems,
):
    section, dp, mp = lax.axis_index("section"), lax.axis_index("dp"), lax.axis_index("mp")
    zh, y = lax.div(dp, RING), lax.rem(dp, RING)
    x, core = lax.div(mp, 2), lax.rem(mp, 2)

    def around(at, by):
        return lax.rem(at + by, RING)

    partner = {"section": section + 1 - 2 * lax.rem(section, 2)}
    sibling = {"mp": 2 * x + 1 - core}
    at_x = [{"mp": 2 * around(x, o) + core} for o in range(RING)]
    at_y = [{"dp": RING * zh + around(y, o)} for o in range(RING)]
    at_z = [{"dp": RING * around(zh, o) + y} for o in range(RING)]
    others = [{"dp": lax.rem(dp + o, RING * RING)} for o in FAR_FIRST]
    peers = [partner, sibling, at_x[1], at_x[3]] + others

    started = []
    ids = iter(range(COPIES))

    def names(n):
        return [next(ids) for _ in range(n)]

    def send(src, dst, k, to):
        copy = pltpu.make_async_remote_copy(
            src_ref=src, dst_ref=dst, send_sem=send_sems.at[k], recv_sem=recv_sems.at[k],
            device_id=to, device_id_type=pl.DeviceIdType.MESH,
        )
        copy.start()
        started.append(copy)

    def arrive(dst, k):
        pltpu.make_async_remote_copy(
            src_ref=dst, dst_ref=dst, send_sem=send_sems.at[k], recv_sem=recv_sems.at[k],
            device_id=sibling, device_id_type=pl.DeviceIdType.MESH,
        ).wait_recv()

    load_acts = pltpu.make_async_copy(acts.at[:, :, 0], raw, local_sems.at[0])
    load_w = pltpu.make_async_copy(weight, w, local_sems.at[1])
    load_ct = pltpu.make_async_copy(cotan, ct_raw, local_sems.at[2])
    load_gain = pltpu.make_async_copy(gain_hbm, gain_ref, local_sems.at[4])
    load_shift = pltpu.make_async_copy(shift_hbm, shift_ref, local_sems.at[5])
    load_acts.start()
    load_ct.start()
    load_w.start()
    load_gain.start()
    load_shift.start()
    barrier = pltpu.get_barrier_semaphore()
    for peer in peers:
        pl.semaphore_signal(barrier, inc=1, device_id=peer, device_id_type=pl.DeviceIdType.MESH)
    strips[:, 14:TILE, :] = jnp.zeros((STRIPS, TILE - 14, CH), BF16)
    ct_strips[...] = jnp.zeros_like(ct_strips)
    choose = picks(2)
    load_acts.wait()
    strips[:, 0:14, :] = raw[...].reshape(STRIPS, 14, CH)
    own[...] = dot(choose, strips[...].reshape(STRIPS * TILE, CH), (1, 0)).astype(BF16)
    pl.semaphore_wait(barrier, len(peers))

    size = PAD // PARTS
    parts = [pl.ds(p * size, size) for p in range(PARTS)]
    k_part, k_left, k_right, k_sib = names(PARTS), names(PARTS), names(PARTS), names(PARTS)
    k_sl, k_sr, k_so, k_opp = names(PARTS), names(PARTS), names(PARTS), names(PARTS)
    for p in range(PARTS):
        send(own.at[parts[p]], full.at[x, core, parts[p]], k_part[p], partner)
    for p in range(PARTS):
        here = full.at[x, core, parts[p]]
        arrive(here, k_part[p])
        send(here, here, k_right[p], at_x[1])
        send(here, here, k_left[p], at_x[3])
        send(here, here, k_sib[p], sibling)
        if p == 0:
            load_ct.wait()
            ct_strips[:, 0:7, :] = ct_raw[...].reshape(STRIPS, 7, COLS)
            cot[...] = dot(picks(1), ct_strips[...].reshape(STRIPS * TILE, COLS), (1, 0))
            pick[...] = picks(1, back=True)
            load_w.wait()
            load_gain.wait()
            load_shift.wait()

    def w_block(xx, cc):
        return w[pl.ds(pl.multiple_of(CH * (2 * xx + cc), CH), CH), :]

    def term(xx, cc):
        return dot(full[xx, cc], w_block(xx, cc), (1, 0))

    k_ex, k_es = [names(3) for _ in range(RING)], names(3)
    my_rows = pl.ds(pl.multiple_of(HALF * core, HALF), HALF)

    def quarter(xx, yy, rows):
        return full.at[xx, lax.div(yy, 2), rows, pl.ds(pl.multiple_of(COLS * lax.rem(yy, 2), COLS), COLS)]

    def ex_rows(yy, cc):
        return pl.ds(pl.multiple_of(PAD * yy + HALF * cc, HALF), HALF)

    def exchange(slot, xx):
        for o in (2, 1, 3):
            yy = around(y, o)
            send(quarter(xx, yy, my_rows), ex.at[xx, ex_rows(y, core)], k_ex[slot][o - 1], at_y[o])

    lx, rx, ox = around(x, 3), around(x, 1), around(x, 2)
    for p in range(PARTS):
        from_left = full.at[lx, core, parts[p]]
        arrive(from_left, k_right[p])
        if p < PARTS // 2:
            send(from_left, from_left, k_opp[p], at_x[1])
        send(from_left, from_left, k_sl[p], sibling)
        from_right = full.at[rx, core, parts[p]]
        arrive(from_right, k_left[p])
        if p >= PARTS // 2:
            send(from_right, from_right, k_opp[p], at_x[3])
        send(from_right, from_right, k_sr[p], sibling)
        if p == 0:
            for q in range(PARTS):
                arrive(full.at[x, 1 - core, parts[q]], k_sib[q])
            exchange(0, x)
    hid[...] = term(x, core)
    hid[...] += term(x, 1 - core)
    hid[...] += term(lx, core)
    hid[...] += term(rx, core)
    for p in range(PARTS):
        arrive(full.at[lx, 1 - core, parts[p]], k_sl[p])
        arrive(full.at[rx, 1 - core, parts[p]], k_sr[p])
    exchange(1, lx)
    exchange(3, rx)
    hid[...] += term(lx, 1 - core)
    hid[...] += term(rx, 1 - core)
    for p in range(PARTS):
        opposite = full.at[ox, core, parts[p]]
        arrive(opposite, k_opp[p])
        send(opposite, opposite, k_so[p], sibling)
    hid[...] += term(ox, core)
    for p in range(PARTS):
        arrive(full.at[ox, 1 - core, parts[p]], k_so[p])
    hid[...] += term(ox, 1 - core)

    def tell(buf, a, b, ks):
        first = lax.broadcasted_iota(jnp.int32, (2, COLS), 0) == 0
        buf[dp] = jnp.where(first, a, b)
        for k, to in zip(ks, others):
            send(buf.at[dp], buf.at[dp], k, to)

    def hear(buf, ks):
        for k, o in zip(ks, FAR_FIRST):
            arrive(buf.at[lax.rem(dp + RING * RING - o, RING * RING)], k)
        return buf[...]

    bands = [pl.ds(b * BAND, BAND) for b in range(PAD // BAND)]
    mean = sum(jnp.sum(hid[band, :], axis=0, keepdims=True) for band in bands) / ROWS
    square = jnp.zeros_like(mean)
    for b, band in enumerate(bands):
        off = hid[band, :] - mean
        if (b + 1) * BAND > ROWS:
            row = lax.broadcasted_iota(jnp.int32, (BAND, COLS), 0)
            off = jnp.where(row < ROWS - b * BAND, off, 0.0)
        square += jnp.sum(off * off, axis=0, keepdims=True)
    k_stat, k_grad = names(15), names(15)
    tell(stat, mean, square, k_stat)
    exchange(2, ox)
    keep = pltpu.make_async_copy(
        full.at[:, lax.div(y, 2), :, pl.ds(pl.multiple_of(COLS * lax.rem(y, 2), COLS), COLS)],
        ex.at[:, pl.ds(pl.multiple_of(PAD * y, PAD), PAD), :],
        local_sems.at[3],
    )
    keep.start()

    heard = hear(stat, k_stat)
    means = heard[:, 0:1, :]
    mean = jnp.sum(means, axis=0) / (RING * RING)
    square = jnp.sum(heard[:, 1:2, :] + ROWS * (means - mean) * (means - mean), axis=0)
    total = float(ROWS * RING * RING)
    inverse = lax.rsqrt(square / total + 1e-05)
    gain, shift = gain_ref[...], shift_ref[...]
    d_bias, d_gain = jnp.zeros_like(mean), jnp.zeros_like(mean)
    for band in bands:
        normed = (hid[band, :] - mean) * inverse
        pre_act = gain * normed + shift
        squash = 0.5 * jnp.tanh(0.5 * pre_act) + 0.5
        acted[band, :] = (pre_act * squash).astype(BF16)
        grad_pre = cot[band, :] * (squash * (1.0 + pre_act * (1.0 - squash)))
        cot[band, :] = grad_pre
        d_bias += jnp.sum(grad_pre, axis=0, keepdims=True)
        d_gain += jnp.sum(grad_pre * normed, axis=0, keepdims=True)
    tell(grad, d_bias, d_gain, k_grad)

    for o in (1, 3, 2):
        rows = ex_rows(around(y, RING - o), core)
        for slot, xx in enumerate((x, lx, ox, rx)):
            arrive(ex.at[xx, rows], k_ex[slot][o - 1])
        send(ex.at[:, rows], ex.at[:, rows], k_es[o - 1], sibling)

    sums = jnp.sum(hear(grad, k_grad), axis=0)
    d_bias, d_gain = sums[0:1, :], sums[1:2, :]
    scale = gain * inverse
    less, tilt = d_bias / total, inverse * (d_gain / total)
    for band in bands:
        part = scale * (cot[band, :] - less - (hid[band, :] - mean) * tilt)
        mine[band, :] = part.astype(BF16)

    k_up, k_down, k_far = names(4), names(4), names(4)
    order = (2, 1, 3, 0)

    def gh_rows(j, yy, h):
        return gh.at[j, pl.ds(pl.multiple_of(PAD * yy + HALF * h, HALF), HALF), :]

    for j in range(2):
        gh[j, pl.ds(pl.multiple_of(PAD * y, PAD), PAD), :] = mine[:, HALF * j : HALF * (j + 1)]
        for h in range(2):
            send(gh_rows(j, y, h), gh_rows(j, y, h), k_up[2 * j + h], at_y[1])
            send(gh_rows(j, y, 1 - h), gh_rows(j, y, 1 - h), k_down[2 * j + 1 - h], at_y[3])

    k_cs = names(4)
    for o in order:
        to_sib[o] = dot(mine[...], w_block(around(x, o), 1 - core), (1, 1)).astype(BF16)
        send(to_sib.at[o], from_sib.at[o], k_cs[o], sibling)

    ly, ry, oy = around(y, 3), around(y, 1), around(y, 2)
    for j in range(2):
        arrive(gh_rows(j, ly, 0), k_up[2 * j])
        send(gh_rows(j, ly, 0), gh_rows(j, ly, 0), k_far[2 * j], at_y[1])
        arrive(gh_rows(j, ry, 1), k_down[2 * j + 1])
        send(gh_rows(j, ry, 1), gh_rows(j, ry, 1), k_far[2 * j + 1], at_y[3])

    def ring_start(block, opp, left, right, to, ks):
        mid = block.shape[1] // 2
        lo, hi = pl.ds(0, mid), pl.ds(mid, mid)
        send(block.at[2, lo], opp.at[lo], ks[0], to[1])
        send(block.at[2, hi], opp.at[hi], ks[1], to[3])
        send(block.at[1, hi], left.at[hi], ks[2], to[1])
        send(block.at[3, lo], right.at[lo], ks[3], to[3])

    def ring_middle(block, opp, left, right, to, ks):
        mid = block.shape[1] // 2
        lo, hi = pl.ds(0, mid), pl.ds(mid, mid)
        arrive(opp.at[lo], ks[0])
        block[1, lo] = (block[1, lo].astype(F32) + opp[lo].astype(F32)).astype(BF16)
        send(block.at[1, lo], left.at[lo], ks[4], to[1])
        arrive(opp.at[hi], ks[1])
        block[3, hi] = (block[3, hi].astype(F32) + opp[hi].astype(F32)).astype(BF16)
        send(block.at[3, hi], right.at[hi], ks[5], to[3])

    def ring_end(block, left, right, ks):
        mid = block.shape[1] // 2
        lo, hi = pl.ds(0, mid), pl.ds(mid, mid)
        arrive(left.at[hi], ks[2])
        arrive(right.at[lo], ks[3])
        arrive(left.at[lo], ks[4])
        arrive(right.at[hi], ks[5])
        return block[0].astype(F32) + left[...].astype(F32) + right[...].astype(F32)

    k_x, k_z, k_back = names(6), [names(6), names(6)], names(1)
    for o in order:
        part = dot(mine[...], w_block(around(x, o), core), (1, 1))
        arrive(from_sib.at[o], k_cs[o])
        xb[o] = (part + from_sib[o].astype(F32)).astype(BF16)
    ring_x = (xb, x_opp, x_left, x_right)
    ring_start(*ring_x, at_x, k_x)

    keep.wait()
    for o in (1, 3, 2):
        rows = ex_rows(around(y, RING - o), 1 - core)
        arrive(ex.at[:, rows], k_es[o - 1])
    ring_z = [[ref.at[j] for ref in (zb, z_opp, z_left, z_right)] for j in range(2)]
    for j in range(2):
        arrive(gh_rows(j, ly, 1), k_up[2 * j + 1])
        arrive(gh_rows(j, ry, 0), k_down[2 * j])
        arrive(gh_rows(j, oy, 0), k_far[2 * j])
        arrive(gh_rows(j, oy, 1), k_far[2 * j + 1])
        across = gh[j].T
        for o in order:
            zb[j, o] = dot(across, ex[around(zh, o)], (1, 0)).astype(BF16)
        ring_start(*ring_z[j], at_z, k_z[j])

    spaced = dot(pick[...], acted[...], (1, 0)).reshape(STRIPS, TILE, COLS)
    block_out[...] = spaced[:, 0:7, :].astype(BF16)
    bias_grad[...] = d_bias
    gain_grad[...] = d_gain

    ring_middle(*ring_x, at_x, k_x)
    ring_middle(*ring_z[0], at_z, k_z[0])
    share[...] = ring_end(xb, x_left, x_right, k_x).astype(BF16)
    send(share, returned, k_back[0], partner)
    ring_middle(*ring_z[1], at_z, k_z[1])
    for j in range(2):
        block, _, left, right = ring_z[j]
        grad_weight[:, HALF * j : HALF * (j + 1)] = ring_end(block, left, right, k_z[j]).T.astype(BF16)

    arrive(returned, k_back[0])
    spaced = dot(pick[...], returned[...], (1, 0)).reshape(STRIPS, TILE, CH)
    grad_input[...] = spaced[:, 0:7, :].astype(BF16)
    for copy in started:
        copy.wait_send()


def on_device(activations, conv_weight, norm_gain, norm_bias, cotangent):
    images = activations.shape[1]
    acts = activations.reshape(images, 7, 2, 14, CH)
    cotan = cotangent.reshape(images, 7, 7, COLS)
    hbm = pl.BlockSpec(memory_space=pltpu.HBM)
    results = (
        jax.ShapeDtypeStruct((STRIPS, 7, COLS), BF16),
        jax.ShapeDtypeStruct((STRIPS, 7, CH), BF16),
        jax.ShapeDtypeStruct((COLS, COLS), BF16),
        jax.ShapeDtypeStruct((1, COLS), F32),
        jax.ShapeDtypeStruct((1, COLS), F32),
    )
    block_out, grad_input, grad_weight, gain_grad, bias_grad = pl.pallas_call(
        kernel,
        out_shape=results,
        in_specs=[hbm] * 5,
        out_specs=[pl.BlockSpec(memory_space=pltpu.VMEM)] * 5,
        scratch_shapes=[
            pltpu.VMEM((images, 7, 14, CH), BF16),
            pltpu.VMEM((STRIPS, TILE, CH), BF16),
            pltpu.VMEM((RING * 2 * CH, COLS), BF16),
            pltpu.VMEM((1, COLS), F32),
            pltpu.VMEM((1, COLS), F32),
            pltpu.VMEM((images, 7, 7, COLS), BF16),
            pltpu.VMEM((STRIPS, TILE, COLS), BF16),
            pltpu.VMEM((STRIPS * TILE, PAD), BF16),
            pltpu.VMEM((PAD, CH), BF16),
            pltpu.VMEM((RING, 2, PAD, CH), BF16),
            pltpu.VMEM((RING, RING * PAD, COLS), BF16),
            pltpu.VMEM((PAD, COLS), BF16),
            pltpu.VMEM((2, RING * PAD, HALF), BF16),
            pltpu.VMEM((PAD, COLS), F32),
            pltpu.VMEM((PAD, COLS), F32),
            pltpu.VMEM((PAD, COLS), BF16),
            pltpu.VMEM((RING * RING, 2, COLS), F32),
            pltpu.VMEM((RING * RING, 2, COLS), F32),
            pltpu.VMEM((RING, PAD, CH), BF16),
            pltpu.VMEM((RING, PAD, CH), BF16),
            pltpu.VMEM((RING, PAD, CH), BF16),
            pltpu.VMEM((PAD, CH), BF16),
            pltpu.VMEM((PAD, CH), BF16),
            pltpu.VMEM((PAD, CH), BF16),
            pltpu.VMEM((2, RING, HALF, COLS), BF16),
            pltpu.VMEM((2, HALF, COLS), BF16),
            pltpu.VMEM((2, HALF, COLS), BF16),
            pltpu.VMEM((2, HALF, COLS), BF16),
            pltpu.VMEM((PAD, CH), BF16),
            pltpu.VMEM((PAD, CH), BF16),
            pltpu.SemaphoreType.DMA((COPIES,)),
            pltpu.SemaphoreType.DMA((COPIES,)),
            pltpu.SemaphoreType.DMA((6,)),
        ],
        compiler_params=pltpu.CompilerParams(
            collective_id=0, has_side_effects=True, vmem_limit_bytes=VMEM_BYTES
        ),
        name="bottleneck",
    )(*(pltpu.with_memory_space_constraint(a, pltpu.HBM) for a in (acts, conv_weight[0], norm_gain, norm_bias, cotan)))
    return (
        block_out.reshape(1, images, 7, 7, COLS),
        grad_input.reshape(1, images, 7, 7, CH),
        grad_weight[None],
        gain_grad,
        bias_grad,
    )


def solution(mesh):
    placed = (
        P("section", "dp", None, None, "mp"),
        P("section", None, "mp"),
        P("section", "mp"),
        P("section", "mp"),
        P("section", "dp", None, None, "mp"),
    )
    return jax.shard_map(
        on_device,
        mesh=mesh,
        in_specs=placed,
        out_specs=(
            P("section", "dp", None, None, "mp"),
            P("section", "dp", None, None, "mp"),
            P("section", "dp", "mp"),
            P("section", "mp"),
            P("section", "mp"),
        ),
        check_vma=False,
    )
```

```python
import functools

import jax
import jax.numpy as jnp
from jax import lax
from jax.experimental import pallas as pl
from jax.experimental.pallas import tpu as pltpu
from jax.sharding import PartitionSpec as P

BF16 = jnp.bfloat16
F32 = jnp.float32
RING = 4
ROWS = 245
PAD = 256
HALF = PAD // 2
CH = 512
COLS = 256
TILE = 16
STRIPS = 35
COPIES = 160
FAR_FIRST = (8, 7, 9, 6, 10, 5, 11, 4, 12, 3, 13, 2, 14, 1, 15)
BAND = 64
PARTS = 4
VMEM_BYTES = 40 * 2**20


def dot(a, b, over):
    return lax.dot_general(a, b, ((over[:1], over[1:]), ((), ())), preferred_element_type=F32)


def picks(step, back=False, rows=(0, PAD), strips=(0, STRIPS)):
    shape = (rows[1] - rows[0], (strips[1] - strips[0]) * TILE)
    shape = shape[::-1] if back else shape
    row = rows[0] + lax.broadcasted_iota(jnp.int32, shape, 1 if back else 0)
    col = strips[0] * TILE + lax.broadcasted_iota(jnp.int32, shape, 0 if back else 1)
    pixel = col & (TILE - 1)
    wanted = 7 * (col >> 4) + (pixel if step == 1 else pixel >> 1)
    keep = (row == wanted) & (pixel < 7 * step)
    if step == 2:
        keep = keep & ((pixel & 1) == 0)
    return jnp.where(keep, 1.0, 0.0).astype(F32).astype(BF16)


def kernel(
    acts, weight, gain_hbm, shift_hbm, cotan,
    block_out, grad_input, grad_weight, grads,
    raw, strips, w, gain_ref, shift_ref, ct_raw, ct_strips, pick, own, full, ex, own_rows, mine, gh, hid, cot, acted,
    stat, grad,
    to_sib, from_sib, xb, x_opp, x_left, x_right,
    zb, z_opp, z_left, z_right, share, returned,
    send_sems, recv_sems, local_sems, met_sem,
):
    section, dp, mp = lax.axis_index("section"), lax.axis_index("dp"), lax.axis_index("mp")
    zh, y = lax.div(dp, RING), lax.rem(dp, RING)
    x, core = lax.div(mp, 2), lax.rem(mp, 2)

    def around(at, by):
        return lax.rem(at + by, RING)

    partner = {"section": section + 1 - 2 * lax.rem(section, 2)}
    sibling = {"mp": 2 * x + 1 - core}
    at_x = [{"mp": 2 * around(x, o) + core} for o in range(RING)]
    at_y = [{"dp": RING * zh + around(y, o)} for o in range(RING)]
    at_z = [{"dp": RING * around(zh, o) + y} for o in range(RING)]
    others = [{"dp": lax.rem(dp + o, RING * RING)} for o in FAR_FIRST]
    near = [partner, at_x[1], at_x[3]] + at_y[1:]
    far = [{"dp": RING * around(zh, i) + around(y, j)} for i in (2, 1, 3) for j in range(RING)]

    started = []
    ids = iter(range(COPIES))

    def names(n):
        return [next(ids) for _ in range(n)]

    def send(src, dst, k, to):
        copy = pltpu.make_async_remote_copy(
            src_ref=src, dst_ref=dst, send_sem=send_sems.at[k], recv_sem=recv_sems.at[k],
            device_id=to, device_id_type=pl.DeviceIdType.MESH,
        )
        copy.start()
        started.append(copy)

    def arrive(dst, k):
        pltpu.make_async_remote_copy(
            src_ref=dst, dst_ref=dst, send_sem=send_sems.at[k], recv_sem=recv_sems.at[k],
            device_id=sibling, device_id_type=pl.DeviceIdType.MESH,
        ).wait_recv()

    early = 2
    load_first = pltpu.make_async_copy(acts.at[0:early, :, 0], raw.at[0:early], local_sems.at[0])
    load_rest = pltpu.make_async_copy(acts.at[early:, :, 0], raw.at[early:], local_sems.at[6])
    load_w = pltpu.make_async_copy(weight, w, local_sems.at[1])
    load_ct = pltpu.make_async_copy(cotan, ct_raw, local_sems.at[2])
    load_gain = pltpu.make_async_copy(gain_hbm, gain_ref, local_sems.at[4])
    load_shift = pltpu.make_async_copy(shift_hbm, shift_ref, local_sems.at[5])
    load_first.start()
    load_rest.start()
    load_ct.start()
    load_w.start()
    load_gain.start()
    load_shift.start()
    barrier = pltpu.get_barrier_semaphore()

    def signal(sem, to):
        pl.semaphore_signal(sem, inc=1, device_id=to, device_id_type=pl.DeviceIdType.MESH)

    @pl.when(core == 1)
    def _():
        signal(barrier, sibling)

    for to in near:
        signal(barrier, {"mp": 2 * x, **to, **({"mp": to["mp"] - core} if "mp" in to else {})})
    for to in far:
        signal(barrier, {"mp": 2 * x + 1, **to})
    strips[:, 14:TILE, :] = jnp.zeros((STRIPS, TILE - 14, CH), BF16)
    size = PAD // PARTS
    parts = [pl.ds(p * size, size) for p in range(PARTS)]

    def sample(p):
        first, last = p * size // 7, min(((p + 1) * size - 1) // 7 + 1, STRIPS)
        choose = picks(2, rows=(p * size, (p + 1) * size), strips=(first, last))
        pixels = strips[first:last].reshape((last - first) * TILE, CH)
        own[parts[p], :] = dot(choose, pixels, (1, 0)).astype(BF16)

    load_first.wait()
    strips[0 : 7 * early, 0:14, :] = raw[0:early].reshape(7 * early, 14, CH)
    sample(0)
    @pl.when(core == 0)
    def _():
        pl.semaphore_wait(barrier, 2 * len(near) + 1)
        signal(met_sem, sibling)

    @pl.when(core == 1)
    def _():
        pl.semaphore_wait(met_sem, 1)


    k_part, k_left, k_right, k_sib = names(PARTS), names(PARTS), names(PARTS), names(PARTS)
    k_sl, k_sr, k_so, k_opp = names(PARTS), names(PARTS), names(PARTS), names(PARTS)
    for p in range(PARTS):
        if p == 1:
            load_rest.wait()
            strips[7 * early :, 0:14, :] = raw[early:].reshape(STRIPS - 7 * early, 14, CH)
        if p > 0:
            sample(p)
        send(own.at[parts[p]], full.at[x, core, parts[p]], k_part[p], partner)
    ct_strips[...] = jnp.zeros_like(ct_strips)
    for p in range(PARTS):
        here = full.at[x, core, parts[p]]
        arrive(here, k_part[p])
        send(here, here, k_right[p], at_x[1])
        send(here, here, k_left[p], at_x[3])
        send(here, here, k_sib[p], sibling)
        if p == 0:
            load_ct.wait()
            ct_strips[:, 0:7, :] = ct_raw[...].reshape(STRIPS, 7, COLS)
            cot[...] = dot(picks(1), ct_strips[...].reshape(STRIPS * TILE, COLS), (1, 0))
            pick[...] = picks(1, back=True)
            load_w.wait()
            load_gain.wait()
            load_shift.wait()

    def w_block(xx, cc):
        return w[pl.ds(pl.multiple_of(CH * (2 * xx + cc), CH), CH), :]

    def term(xx, cc):
        return dot(full[xx, cc], w_block(xx, cc), (1, 0))

    k_ex, k_xl, k_xr, k_xo, k_es = names(RING), names(2), names(2), names(2), names(RING)

    def exchange():
        for o in (2, 1, 3):
            yy = around(y, o)
            at = pl.multiple_of(COLS * lax.rem(yy, 2), COLS)
            rows = pl.ds(pl.multiple_of(HALF * core, HALF), HALF)
            send(
                full.at[x, lax.div(yy, 2), rows, pl.ds(at, COLS)],
                ex.at[x, RING - o, core], k_ex[o], at_y[o],
            )

    def others_of(xx, cc, h=None):
        rows = pl.ds(0, HALF) if h is None else pl.ds(h * BAND, BAND)
        return ex.at[xx, pl.ds(1, RING - 1), cc, rows]

    def along_x():
        for o in range(1, RING):
            arrive(ex.at[x, RING - o, core], k_ex[o])
        for h in range(2):
            send(others_of(x, core, h), others_of(x, core, h), k_xl[h], at_x[1])
            send(others_of(x, core, 1 - h), others_of(x, core, 1 - h), k_xr[1 - h], at_x[3])
        send(others_of(x, core), others_of(x, core), k_es[0], sibling)

    def farther_x():
        arrive(others_of(lx, core, 0), k_xl[0])
        send(others_of(lx, core, 0), others_of(lx, core, 0), k_xo[0], at_x[1])
        arrive(others_of(rx, core, 1), k_xr[1])
        send(others_of(rx, core, 1), others_of(rx, core, 1), k_xo[1], at_x[3])
        arrive(others_of(lx, core, 1), k_xl[1])
        send(others_of(lx, core), others_of(lx, core), k_es[1], sibling)
        arrive(others_of(rx, core, 0), k_xr[0])
        send(others_of(rx, core), others_of(rx, core), k_es[2], sibling)

    def last_x():
        arrive(others_of(ox, core, 0), k_xo[0])
        arrive(others_of(ox, core, 1), k_xo[1])
        send(others_of(ox, core), others_of(ox, core), k_es[3], sibling)

    lx, rx, ox = around(x, 3), around(x, 1), around(x, 2)
    for p in range(PARTS):
        from_left = full.at[lx, core, parts[p]]
        arrive(from_left, k_right[p])
        if p < PARTS // 2:
            send(from_left, from_left, k_opp[p], at_x[1])
        send(from_left, from_left, k_sl[p], sibling)
        from_right = full.at[rx, core, parts[p]]
        arrive(from_right, k_left[p])
        if p >= PARTS // 2:
            send(from_right, from_right, k_opp[p], at_x[3])
        send(from_right, from_right, k_sr[p], sibling)
        if p == 0:
            for q in range(PARTS):
                arrive(full.at[x, 1 - core, parts[q]], k_sib[q])
            exchange()
    hid[...] = term(x, core)
    hid[...] += term(x, 1 - core)
    hid[...] += term(lx, core)
    hid[...] += term(rx, core)
    for p in range(PARTS):
        arrive(full.at[lx, 1 - core, parts[p]], k_sl[p])
        arrive(full.at[rx, 1 - core, parts[p]], k_sr[p])
    hid[...] += term(lx, 1 - core)
    hid[...] += term(rx, 1 - core)
    for p in range(PARTS):
        opposite = full.at[ox, core, parts[p]]
        arrive(opposite, k_opp[p])
        send(opposite, opposite, k_so[p], sibling)
    hid[...] += term(ox, core)
    for p in range(PARTS):
        arrive(full.at[ox, 1 - core, parts[p]], k_so[p])
    hid[...] += term(ox, 1 - core)

    def tell(buf, a, b, ks):
        first = lax.broadcasted_iota(jnp.int32, (2, COLS), 0) == 0
        buf[dp] = jnp.where(first, a, b)
        for k, to in zip(ks, others):
            send(buf.at[dp], buf.at[dp], k, to)

    def hear(buf, ks):
        for k, o in zip(ks, FAR_FIRST):
            arrive(buf.at[lax.rem(dp + RING * RING - o, RING * RING)], k)
        return buf[...]

    bands = [pl.ds(b * BAND, BAND) for b in range(PAD // BAND)]
    mean = sum(jnp.sum(hid[band, :], axis=0, keepdims=True) for band in bands) / ROWS
    square = jnp.zeros_like(mean)
    for b, band in enumerate(bands):
        off = hid[band, :] - mean
        if (b + 1) * BAND > ROWS:
            row = lax.broadcasted_iota(jnp.int32, (BAND, COLS), 0)
            off = jnp.where(row < ROWS - b * BAND, off, 0.0)
        square += jnp.sum(off * off, axis=0, keepdims=True)
    k_stat, k_grad = names(15), names(15)
    @pl.when(core == 1)
    def _():
        pl.semaphore_wait(barrier, 2 * len(far))
        signal(met_sem, sibling)

    @pl.when(core == 0)
    def _():
        pl.semaphore_wait(met_sem, 1)

    tell(stat, mean, square, k_stat)
    along_x()
    keep = pltpu.make_async_copy(
        full.at[:, lax.div(y, 2), :, pl.ds(pl.multiple_of(COLS * lax.rem(y, 2), COLS), COLS)],
        own_rows, local_sems.at[3],
    )
    keep.start()

    heard = hear(stat, k_stat)
    means = heard[:, 0:1, :]
    mean = jnp.sum(means, axis=0) / (RING * RING)
    square = jnp.sum(heard[:, 1:2, :] + ROWS * (means - mean) * (means - mean), axis=0)
    total = float(ROWS * RING * RING)
    inverse = lax.rsqrt(square / total + 1e-05)
    gain, shift = gain_ref[...], shift_ref[...]
    d_bias, d_gain = jnp.zeros_like(mean), jnp.zeros_like(mean)
    for band in bands:
        normed = (hid[band, :] - mean) * inverse
        pre_act = gain * normed + shift
        squash = 0.5 * jnp.tanh(0.5 * pre_act) + 0.5
        acted[band, :] = (pre_act * squash).astype(BF16)
        grad_pre = cot[band, :] * (squash * (1.0 + pre_act * (1.0 - squash)))
        cot[band, :] = grad_pre
        d_bias += jnp.sum(grad_pre, axis=0, keepdims=True)
        d_gain += jnp.sum(grad_pre * normed, axis=0, keepdims=True)
    tell(grad, d_bias, d_gain, k_grad)

    farther_x()
    sums = jnp.sum(hear(grad, k_grad), axis=0)
    d_bias, d_gain = sums[0:1, :], sums[1:2, :]
    scale = gain * inverse
    less, tilt = d_bias / total, inverse * (d_gain / total)
    for band in bands:
        part = scale * (cot[band, :] - less - (hid[band, :] - mean) * tilt)
        mine[band, :] = part.astype(BF16)

    halves = [pl.ds(0, HALF), pl.ds(HALF, HALF)]

    k_up, k_down, k_far = names(4), names(4), names(4)
    order = (2, 1, 3, 0)

    def gh_rows(j, r, h):
        return gh.at[j, pl.ds(PAD * r + HALF * h, HALF), :]

    for j in range(2):
        gh[j, 0:PAD, :] = mine[:, HALF * j : HALF * (j + 1)]
        for h in range(2):
            send(gh_rows(j, 0, h), gh_rows(j, 3, h), k_up[2 * j + h], at_y[1])
            send(gh_rows(j, 0, 1 - h), gh_rows(j, 1, 1 - h), k_down[2 * j + 1 - h], at_y[3])

    k_cs = [names(4), names(4)]
    for q in range(2):
        for o in order:
            part = dot(mine[halves[q], :], w_block(around(x, o), 1 - core), (1, 1))
            to_sib[q, o] = part.astype(BF16)
            send(to_sib.at[q, o], from_sib.at[q, o], k_cs[q][o], sibling)

    last_x()
    for j in range(2):
        arrive(gh_rows(j, 3, 0), k_up[2 * j])
        send(gh_rows(j, 3, 0), gh_rows(j, 2, 0), k_far[2 * j], at_y[1])
        arrive(gh_rows(j, 1, 1), k_down[2 * j + 1])
        send(gh_rows(j, 1, 1), gh_rows(j, 2, 1), k_far[2 * j + 1], at_y[3])

    def ring_start(block, opp, left, right, to, ks):
        mid = block.shape[1] // 2
        lo, hi = pl.ds(0, mid), pl.ds(mid, mid)
        send(block.at[2, lo], opp.at[lo], ks[0], to[1])
        send(block.at[2, hi], opp.at[hi], ks[1], to[3])
        send(block.at[1, hi], left.at[hi], ks[2], to[1])
        send(block.at[3, lo], right.at[lo], ks[3], to[3])

    def ring_middle(block, opp, left, right, to, ks):
        mid = block.shape[1] // 2
        lo, hi = pl.ds(0, mid), pl.ds(mid, mid)
        arrive(opp.at[lo], ks[0])
        block[1, lo] = (block[1, lo].astype(F32) + opp[lo].astype(F32)).astype(BF16)
        send(block.at[1, lo], left.at[lo], ks[4], to[1])
        arrive(opp.at[hi], ks[1])
        block[3, hi] = (block[3, hi].astype(F32) + opp[hi].astype(F32)).astype(BF16)
        send(block.at[3, hi], right.at[hi], ks[5], to[3])

    def ring_end(block, left, right, ks):
        mid = block.shape[1] // 2
        lo, hi = pl.ds(0, mid), pl.ds(mid, mid)
        arrive(left.at[hi], ks[2])
        arrive(right.at[lo], ks[3])
        arrive(left.at[lo], ks[4])
        arrive(right.at[hi], ks[5])
        return block[0].astype(F32) + left[...].astype(F32) + right[...].astype(F32)

    k_x, k_z, k_back = [names(6), names(6)], [names(6), names(6)], names(2)
    ring_x = [[ref.at[q] for ref in (xb, x_opp, x_left, x_right)] for q in range(2)]
    ring_z = [[ref.at[j] for ref in (zb, z_opp, z_left, z_right)] for j in range(2)]

    def start_x(q):
        for o in order:
            part = dot(mine[halves[q], :], w_block(around(x, o), core), (1, 1))
            arrive(from_sib.at[q, o], k_cs[q][o])
            xb[q, o] = (part + from_sib[q, o].astype(F32)).astype(BF16)
        ring_start(*ring_x[q], at_x, k_x[q])

    def start_z(j):
        arrive(gh_rows(j, 3, 1), k_up[2 * j + 1])
        arrive(gh_rows(j, 1, 0), k_down[2 * j])
        arrive(gh_rows(j, 2, 0), k_far[2 * j])
        arrive(gh_rows(j, 2, 1), k_far[2 * j + 1])
        across = gh[j].T
        for o in order:
            slot = around(zh, o)
            rest = ex[slot, 1:RING].reshape((RING - 1) * PAD, COLS)
            block = dot(across[:, 0:PAD], own_rows[slot], (1, 0))
            zb[j, o] = (block + dot(across[:, PAD:], rest, (1, 0))).astype(BF16)
        ring_start(*ring_z[j], at_z, k_z[j])

    def give_back(q):
        block, _, left, right = ring_x[q]
        share[halves[q], :] = ring_end(block, left, right, k_x[q]).astype(BF16)
        send(share.at[halves[q]], returned.at[halves[q]], k_back[q], partner)

    start_x(0)
    keep.wait()
    for i, xx in enumerate((x, lx, rx, ox)):
        arrive(others_of(xx, 1 - core), k_es[i])
    start_z(0)
    start_x(1)
    start_z(1)

    spaced = dot(pick[...], acted[...], (1, 0)).reshape(STRIPS, TILE, COLS)
    block_out[...] = spaced[:, 0:7, :].astype(BF16)
    grads[...] = sums

    ring_middle(*ring_x[0], at_x, k_x[0])
    ring_middle(*ring_z[0], at_z, k_z[0])
    ring_middle(*ring_x[1], at_x, k_x[1])
    give_back(0)
    ring_middle(*ring_z[1], at_z, k_z[1])
    give_back(1)
    for j in range(2):
        block, _, left, right = ring_z[j]
        grad_weight[:, HALF * j : HALF * (j + 1)] = ring_end(block, left, right, k_z[j]).T.astype(BF16)

    for q in range(2):
        arrive(returned.at[halves[q]], k_back[q])
    spaced = dot(pick[...], returned[...], (1, 0)).reshape(STRIPS, TILE, CH)
    grad_input[...] = spaced[:, 0:7, :].astype(BF16)
    for copy in started:
        copy.wait_send()


def on_device(activations, conv_weight, norm_gain, norm_bias, cotangent):
    images = activations.shape[1]
    acts = activations.reshape(images, 7, 2, 14, CH)
    cotan = cotangent.reshape(images, 7, 7, COLS)
    hbm = pl.BlockSpec(memory_space=pltpu.HBM)
    results = (
        jax.ShapeDtypeStruct((STRIPS, 7, COLS), BF16),
        jax.ShapeDtypeStruct((STRIPS, 7, CH), BF16),
        jax.ShapeDtypeStruct((COLS, COLS), BF16),
        jax.ShapeDtypeStruct((2, COLS), F32),
    )
    block_out, grad_input, grad_weight, grads = pl.pallas_call(
        kernel,
        out_shape=results,
        in_specs=[hbm] * 5,
        out_specs=[pl.BlockSpec(memory_space=pltpu.VMEM)] * 4,
        scratch_shapes=[
            pltpu.VMEM((images, 7, 14, CH), BF16),
            pltpu.VMEM((STRIPS, TILE, CH), BF16),
            pltpu.VMEM((RING * 2 * CH, COLS), BF16),
            pltpu.VMEM((1, COLS), F32),
            pltpu.VMEM((1, COLS), F32),
            pltpu.VMEM((images, 7, 7, COLS), BF16),
            pltpu.VMEM((STRIPS, TILE, COLS), BF16),
            pltpu.VMEM((STRIPS * TILE, PAD), BF16),
            pltpu.VMEM((PAD, CH), BF16),
            pltpu.VMEM((RING, 2, PAD, CH), BF16),
            pltpu.VMEM((RING, RING, 2, HALF, COLS), BF16),
            pltpu.VMEM((RING, PAD, COLS), BF16),
            pltpu.VMEM((PAD, COLS), BF16),
            pltpu.VMEM((2, RING * PAD, HALF), BF16),
            pltpu.VMEM((PAD, COLS), F32),
            pltpu.VMEM((PAD, COLS), F32),
            pltpu.VMEM((PAD, COLS), BF16),
            pltpu.VMEM((RING * RING, 2, COLS), F32),
            pltpu.VMEM((RING * RING, 2, COLS), F32),
            pltpu.VMEM((2, RING, HALF, CH), BF16),
            pltpu.VMEM((2, RING, HALF, CH), BF16),
            pltpu.VMEM((2, RING, HALF, CH), BF16),
            pltpu.VMEM((2, HALF, CH), BF16),
            pltpu.VMEM((2, HALF, CH), BF16),
            pltpu.VMEM((2, HALF, CH), BF16),
            pltpu.VMEM((2, RING, HALF, COLS), BF16),
            pltpu.VMEM((2, HALF, COLS), BF16),
            pltpu.VMEM((2, HALF, COLS), BF16),
            pltpu.VMEM((2, HALF, COLS), BF16),
            pltpu.VMEM((PAD, CH), BF16),
            pltpu.VMEM((PAD, CH), BF16),
            pltpu.SemaphoreType.DMA((COPIES,)),
            pltpu.SemaphoreType.DMA((COPIES,)),
            pltpu.SemaphoreType.DMA((7,)),
            pltpu.SemaphoreType.REGULAR,
        ],
        compiler_params=pltpu.CompilerParams(
            collective_id=0, has_side_effects=True, vmem_limit_bytes=VMEM_BYTES
        ),
        name="bottleneck",
    )(*(pltpu.with_memory_space_constraint(a, pltpu.HBM) for a in (acts, conv_weight[0], norm_gain, norm_bias, cotan)))
    return (
        block_out.reshape(1, images, 7, 7, COLS),
        grad_input.reshape(1, images, 7, 7, CH),
        grad_weight[None],
        grads[1:2],
        grads[0:1],
    )


def solution(mesh):
    placed = (
        P("section", "dp", None, None, "mp"),
        P("section", None, "mp"),
        P("section", "mp"),
        P("section", "mp"),
        P("section", "dp", None, None, "mp"),
    )
    return jax.shard_map(
        on_device,
        mesh=mesh,
        in_specs=placed,
        out_specs=(
            P("section", "dp", None, None, "mp"),
            P("section", "dp", None, None, "mp"),
            P("section", "dp", "mp"),
            P("section", "mp"),
            P("section", "mp"),
        ),
        check_vma=False,
    )
```

```python
import functools

import jax
import jax.numpy as jnp
from jax import lax
from jax.experimental import pallas as pl
from jax.experimental.pallas import tpu as pltpu
from jax.sharding import PartitionSpec as P

BF16 = jnp.bfloat16
F32 = jnp.float32
RING = 4
ROWS = 245
PAD = 256
HALF = PAD // 2
CH = 512
COLS = 256
TILE = 16
STRIPS = 35
COPIES = 160
FAR_FIRST = (8, 7, 9, 6, 10, 5, 11, 4, 12, 3, 13, 2, 14, 1, 15)
BAND = 64
CUTS = ((0, 128), (128, 256))
PARTS = 4
VMEM_BYTES = 40 * 2**20


def dot(a, b, over):
    return lax.dot_general(a, b, ((over[:1], over[1:]), ((), ())), preferred_element_type=F32)


def picks(step, back=False, rows=(0, PAD), strips=(0, STRIPS)):
    shape = (rows[1] - rows[0], (strips[1] - strips[0]) * TILE)
    shape = shape[::-1] if back else shape
    row = rows[0] + lax.broadcasted_iota(jnp.int32, shape, 1 if back else 0)
    col = strips[0] * TILE + lax.broadcasted_iota(jnp.int32, shape, 0 if back else 1)
    pixel = col & (TILE - 1)
    wanted = 7 * (col >> 4) + (pixel if step == 1 else pixel >> 1)
    keep = (row == wanted) & (pixel < 7 * step)
    if step == 2:
        keep = keep & ((pixel & 1) == 0)
    return jnp.where(keep, 1.0, 0.0).astype(F32).astype(BF16)


def kernel(
    acts, weight, gain_hbm, shift_hbm, cotan,
    block_out, grad_input, grad_weight, grads,
    raw, strips, w, gain_ref, shift_ref, ct_raw, ct_strips, pick, own, full, ex, own_rows, mine, across, hid, cot, acted,
    stat, grad,
    w_mate, mate, xb, x_opp, x_left, x_right,
    zb, z_opp, z_left, z_right, share, returned,
    send_sems, recv_sems, local_sems, met_sem,
):
    section, dp, mp = lax.axis_index("section"), lax.axis_index("dp"), lax.axis_index("mp")
    zh, y = lax.div(dp, RING), lax.rem(dp, RING)
    x, core = lax.div(mp, 2), lax.rem(mp, 2)

    def around(at, by):
        return lax.rem(at + by, RING)

    partner = {"section": section + 1 - 2 * lax.rem(section, 2)}
    sibling = {"mp": 2 * x + 1 - core}
    at_x = [{"mp": 2 * around(x, o) + core} for o in range(RING)]
    at_y = [{"dp": RING * zh + around(y, o)} for o in range(RING)]
    at_z = [{"dp": RING * around(zh, o) + y} for o in range(RING)]
    others = [{"dp": lax.rem(dp + o, RING * RING)} for o in FAR_FIRST]
    near = [partner, at_x[1], at_x[3]] + at_y[1:]
    far = [{"dp": RING * around(zh, i) + around(y, j)} for i in (2, 1, 3) for j in range(RING)]

    started = []
    ids = iter(range(COPIES))

    def names(n):
        return [next(ids) for _ in range(n)]

    def send(src, dst, k, to):
        copy = pltpu.make_async_remote_copy(
            src_ref=src, dst_ref=dst, send_sem=send_sems.at[k], recv_sem=recv_sems.at[k],
            device_id=to, device_id_type=pl.DeviceIdType.MESH,
        )
        copy.start()
        started.append(copy)

    def arrive(dst, k):
        pltpu.make_async_remote_copy(
            src_ref=dst, dst_ref=dst, send_sem=send_sems.at[k], recv_sem=recv_sems.at[k],
            device_id=sibling, device_id_type=pl.DeviceIdType.MESH,
        ).wait_recv()

    early = 2
    load_first = pltpu.make_async_copy(acts.at[0:early, :, 0], raw.at[0:early], local_sems.at[0])
    load_rest = pltpu.make_async_copy(acts.at[early:, :, 0], raw.at[early:], local_sems.at[6])
    load_w = pltpu.make_async_copy(weight, w, local_sems.at[1])
    load_ct = pltpu.make_async_copy(cotan, ct_raw, local_sems.at[2])
    load_gain = pltpu.make_async_copy(gain_hbm, gain_ref, local_sems.at[4])
    load_shift = pltpu.make_async_copy(shift_hbm, shift_ref, local_sems.at[5])
    load_first.start()
    load_rest.start()
    load_ct.start()
    load_w.start()
    load_gain.start()
    load_shift.start()
    barrier = pltpu.get_barrier_semaphore()

    def signal(sem, to):
        pl.semaphore_signal(sem, inc=1, device_id=to, device_id_type=pl.DeviceIdType.MESH)

    @pl.when(core == 1)
    def _():
        signal(barrier, sibling)

    for to in near:
        signal(barrier, {"mp": 2 * x, **to, **({"mp": to["mp"] - core} if "mp" in to else {})})
    for to in far:
        signal(barrier, {"mp": 2 * x + 1, **to})
    strips[:, 14:TILE, :] = jnp.zeros((STRIPS, TILE - 14, CH), BF16)
    size = PAD // PARTS
    parts = [pl.ds(p * size, size) for p in range(PARTS)]

    def sample(p):
        first, last = p * size // 7, min(((p + 1) * size - 1) // 7 + 1, STRIPS)
        choose = picks(2, rows=(p * size, (p + 1) * size), strips=(first, last))
        pixels = strips[first:last].reshape((last - first) * TILE, CH)
        own[parts[p], :] = dot(choose, pixels, (1, 0)).astype(BF16)

    load_first.wait()
    strips[0 : 7 * early, 0:14, :] = raw[0:early].reshape(7 * early, 14, CH)
    sample(0)
    @pl.when(core == 0)
    def _():
        pl.semaphore_wait(barrier, 2 * len(near) + 1)
        signal(met_sem, sibling)

    @pl.when(core == 1)
    def _():
        pl.semaphore_wait(met_sem, 1)


    k_part, k_left, k_right, k_sib = names(PARTS), names(PARTS), names(PARTS), names(PARTS)
    k_sl, k_sr, k_so, k_opp = names(PARTS), names(PARTS), names(PARTS), names(PARTS)
    for p in range(PARTS):
        if p == 1:
            load_rest.wait()
            strips[7 * early :, 0:14, :] = raw[early:].reshape(STRIPS - 7 * early, 14, CH)
        if p > 0:
            sample(p)
        send(own.at[parts[p]], full.at[x, core, parts[p]], k_part[p], partner)
    ct_strips[...] = jnp.zeros_like(ct_strips)
    for p in range(PARTS):
        here = full.at[x, core, parts[p]]
        arrive(here, k_part[p])
        send(here, here, k_right[p], at_x[1])
        send(here, here, k_left[p], at_x[3])
        send(here, here, k_sib[p], sibling)
        if p == 0:
            load_ct.wait()
            ct_strips[:, 0:7, :] = ct_raw[...].reshape(STRIPS, 7, COLS)
            cot[...] = dot(picks(1), ct_strips[...].reshape(STRIPS * TILE, COLS), (1, 0))
            pick[...] = picks(1, back=True)
            load_w.wait()
            load_gain.wait()
            load_shift.wait()

    def w_block(xx, cc):
        return w[pl.ds(pl.multiple_of(CH * (2 * xx + cc), CH), CH), :]

    def term(xx, cc):
        return dot(full[xx, cc], w_block(xx, cc), (1, 0))

    k_ex, k_xl, k_xr, k_xo, k_es = names(RING), names(2), names(2), names(2), names(RING)

    def exchange():
        for o in (2, 1, 3):
            yy = around(y, o)
            at = pl.multiple_of(COLS * lax.rem(yy, 2), COLS)
            rows = pl.ds(pl.multiple_of(HALF * core, HALF), HALF)
            send(
                full.at[x, lax.div(yy, 2), rows, pl.ds(at, COLS)],
                ex.at[x, RING - o, core], k_ex[o], at_y[o],
            )

    def others_of(xx, cc, h=None):
        rows = pl.ds(0, HALF) if h is None else pl.ds(h * BAND, BAND)
        return ex.at[xx, pl.ds(1, RING - 1), cc, rows]

    def along_x():
        for o in range(1, RING):
            arrive(ex.at[x, RING - o, core], k_ex[o])
        for h in range(2):
            send(others_of(x, core, h), others_of(x, core, h), k_xl[h], at_x[1])
            send(others_of(x, core, 1 - h), others_of(x, core, 1 - h), k_xr[1 - h], at_x[3])
        send(others_of(x, core), others_of(x, core), k_es[0], sibling)

    def farther_x():
        arrive(others_of(lx, core, 0), k_xl[0])
        send(others_of(lx, core, 0), others_of(lx, core, 0), k_xo[0], at_x[1])
        arrive(others_of(rx, core, 1), k_xr[1])
        send(others_of(rx, core, 1), others_of(rx, core, 1), k_xo[1], at_x[3])
        arrive(others_of(lx, core, 1), k_xl[1])
        send(others_of(lx, core), others_of(lx, core), k_es[1], sibling)
        arrive(others_of(rx, core, 0), k_xr[0])
        send(others_of(rx, core), others_of(rx, core), k_es[2], sibling)

    def last_x():
        arrive(others_of(ox, core, 0), k_xo[0])
        arrive(others_of(ox, core, 1), k_xo[1])
        send(others_of(ox, core), others_of(ox, core), k_es[3], sibling)

    lx, rx, ox = around(x, 3), around(x, 1), around(x, 2)
    for p in range(PARTS):
        from_left = full.at[lx, core, parts[p]]
        arrive(from_left, k_right[p])
        if p < PARTS // 2:
            send(from_left, from_left, k_opp[p], at_x[1])
        send(from_left, from_left, k_sl[p], sibling)
        from_right = full.at[rx, core, parts[p]]
        arrive(from_right, k_left[p])
        if p >= PARTS // 2:
            send(from_right, from_right, k_opp[p], at_x[3])
        send(from_right, from_right, k_sr[p], sibling)
        if p == 0:
            for q in range(PARTS):
                arrive(full.at[x, 1 - core, parts[q]], k_sib[q])
            exchange()
    hid[...] = term(x, core)
    hid[...] += term(x, 1 - core)
    hid[...] += term(lx, core)
    hid[...] += term(rx, core)
    for p in range(PARTS):
        arrive(full.at[lx, 1 - core, parts[p]], k_sl[p])
        arrive(full.at[rx, 1 - core, parts[p]], k_sr[p])
    hid[...] += term(lx, 1 - core)
    hid[...] += term(rx, 1 - core)
    for p in range(PARTS):
        opposite = full.at[ox, core, parts[p]]
        arrive(opposite, k_opp[p])
        send(opposite, opposite, k_so[p], sibling)
    hid[...] += term(ox, core)
    for p in range(PARTS):
        arrive(full.at[ox, 1 - core, parts[p]], k_so[p])
    hid[...] += term(ox, 1 - core)

    def tell(buf, a, b, ks):
        first = lax.broadcasted_iota(jnp.int32, (2, COLS), 0) == 0
        buf[dp] = jnp.where(first, a, b)
        for k, to in zip(ks, others):
            send(buf.at[dp], buf.at[dp], k, to)

    def hear(buf, ks):
        for k, o in zip(ks, FAR_FIRST):
            arrive(buf.at[lax.rem(dp + RING * RING - o, RING * RING)], k)
        return buf[...]

    bands = [pl.ds(b * BAND, BAND) for b in range(PAD // BAND)]
    mean = sum(jnp.sum(hid[band, :], axis=0, keepdims=True) for band in bands) / ROWS
    square = jnp.zeros_like(mean)
    for b, band in enumerate(bands):
        off = hid[band, :] - mean
        if (b + 1) * BAND > ROWS:
            row = lax.broadcasted_iota(jnp.int32, (BAND, COLS), 0)
            off = jnp.where(row < ROWS - b * BAND, off, 0.0)
        square += jnp.sum(off * off, axis=0, keepdims=True)
    k_stat, k_grad = names(15), names(15)
    @pl.when(core == 1)
    def _():
        pl.semaphore_wait(barrier, 2 * len(far))
        signal(met_sem, sibling)

    @pl.when(core == 0)
    def _():
        pl.semaphore_wait(met_sem, 1)

    tell(stat, mean, square, k_stat)
    along_x()
    k_w = names(RING)
    for xx in range(RING):
        send(w.at[pl.ds(pl.multiple_of(CH * (2 * xx + 1 - core), CH), CH), :], w_mate.at[xx], k_w[xx], sibling)
    keep = pltpu.make_async_copy(
        full.at[:, lax.div(y, 2), :, pl.ds(pl.multiple_of(COLS * lax.rem(y, 2), COLS), COLS)],
        own_rows, local_sems.at[3],
    )
    keep.start()

    heard = hear(stat, k_stat)
    means = heard[:, 0:1, :]
    mean = jnp.sum(means, axis=0) / (RING * RING)
    square = jnp.sum(heard[:, 1:2, :] + ROWS * (means - mean) * (means - mean), axis=0)
    total = float(ROWS * RING * RING)
    inverse = lax.rsqrt(square / total + 1e-05)
    gain, shift = gain_ref[...], shift_ref[...]
    d_bias, d_gain = jnp.zeros_like(mean), jnp.zeros_like(mean)
    for band in bands:
        normed = (hid[band, :] - mean) * inverse
        pre_act = gain * normed + shift
        squash = 0.5 * jnp.tanh(0.5 * pre_act) + 0.5
        acted[band, :] = (pre_act * squash).astype(BF16)
        grad_pre = cot[band, :] * (squash * (1.0 + pre_act * (1.0 - squash)))
        cot[band, :] = grad_pre
        d_bias += jnp.sum(grad_pre, axis=0, keepdims=True)
        d_gain += jnp.sum(grad_pre * normed, axis=0, keepdims=True)
    tell(grad, d_bias, d_gain, k_grad)

    farther_x()
    sums = jnp.sum(hear(grad, k_grad), axis=0)
    d_bias, d_gain = sums[0:1, :], sums[1:2, :]
    scale = gain * inverse
    less, tilt = d_bias / total, inverse * (d_gain / total)
    for band in bands:
        part = scale * (cot[band, :] - less - (hid[band, :] - mean) * tilt)
        mine[band, :] = part.astype(BF16)

    halves = [pl.ds(0, HALF), pl.ds(HALF, HALF)]

    k_y = [names(RING) for _ in CUTS]
    order = (2, 1, 3, 0)

    def across_from(j, r):
        return across.at[pl.ds(CUTS[j][0], CUTS[j][1] - CUTS[j][0]), pl.ds(PAD * r, PAD)]

    k_mate = names(2)
    for q in range(2):
        send(mine.at[halves[q]], mate.at[halves[q]], k_mate[q], sibling)
    across[:, 0:PAD] = mine[...].T
    for j in range(len(CUTS)):
        for o in (2, 1, 3):
            send(across_from(j, 0), across_from(j, RING - o), k_y[j][o], at_y[o])

    last_x()

    def ring_start(block, opp, left, right, to, ks, cut, make):
        lo, hi = pl.ds(cut[0], (cut[1] - cut[0]) // 2), pl.ds((cut[0] + cut[1]) // 2, (cut[1] - cut[0]) // 2)
        make(2)
        send(block.at[2, lo], opp.at[lo], ks[0], to[1])
        send(block.at[2, hi], opp.at[hi], ks[1], to[3])
        make(1)
        send(block.at[1, hi], left.at[hi], ks[2], to[1])
        make(3)
        send(block.at[3, lo], right.at[lo], ks[3], to[3])
        make(0)

    def ring_middle(block, opp, left, right, to, ks, cut):
        lo, hi = pl.ds(cut[0], (cut[1] - cut[0]) // 2), pl.ds((cut[0] + cut[1]) // 2, (cut[1] - cut[0]) // 2)
        arrive(opp.at[lo], ks[0])
        block[1, lo] = (block[1, lo].astype(F32) + opp[lo].astype(F32)).astype(BF16)
        send(block.at[1, lo], left.at[lo], ks[4], to[1])
        arrive(opp.at[hi], ks[1])
        block[3, hi] = (block[3, hi].astype(F32) + opp[hi].astype(F32)).astype(BF16)
        send(block.at[3, hi], right.at[hi], ks[5], to[3])

    def ring_end(block, left, right, ks, cut):
        lo, hi = pl.ds(cut[0], (cut[1] - cut[0]) // 2), pl.ds((cut[0] + cut[1]) // 2, (cut[1] - cut[0]) // 2)
        arrive(left.at[hi], ks[2])
        arrive(right.at[lo], ks[3])
        arrive(left.at[lo], ks[4])
        arrive(right.at[hi], ks[5])
        rows = slice(*cut)
        return block[0, rows].astype(F32) + left[rows].astype(F32) + right[rows].astype(F32)

    k_x, k_z, k_back = [names(6), names(6)], [names(6) for _ in CUTS], names(2)
    ring_x = (xb, x_opp, x_left, x_right, at_x)
    ring_z = (zb, z_opp, z_left, z_right, at_z)
    cut_x = ((0, HALF), (HALF, PAD))

    def start_x(q):
        def make(o):
            part = dot(mine[halves[q], :], w_block(around(x, o), core), (1, 1))
            part += dot(mate[halves[q], :], w_mate[around(x, o)], (1, 1))
            xb[o, halves[q]] = part.astype(BF16)

        arrive(mate.at[halves[q]], k_mate[q])
        ring_start(*ring_x, k_x[q], cut_x[q], make)

    def start_z(j):
        for o in range(1, RING):
            arrive(across_from(j, RING - o), k_y[j][o])
        rows = slice(*CUTS[j])

        def make(o):
            slot = around(zh, o)
            rest = ex[slot, 1:RING].reshape((RING - 1) * PAD, COLS)
            block = dot(across[rows, 0:PAD], own_rows[slot], (1, 0))
            zb[o, rows] = (block + dot(across[rows, PAD:], rest, (1, 0))).astype(BF16)

        ring_start(*ring_z, k_z[j], CUTS[j], make)

    def give_back(q):
        share[halves[q], :] = ring_end(xb, x_left, x_right, k_x[q], cut_x[q]).astype(BF16)
        send(share.at[halves[q]], returned.at[halves[q]], k_back[q], partner)

    for xx in range(RING):
        arrive(w_mate.at[xx], k_w[xx])
    start_x(0)
    spaced = dot(pick[...], acted[...], (1, 0)).reshape(STRIPS, TILE, COLS)
    block_out[...] = spaced[:, 0:7, :].astype(BF16)
    grads[...] = sums

    keep.wait()
    for i, xx in enumerate((x, lx, rx, ox)):
        arrive(others_of(xx, 1 - core), k_es[i])
    start_z(0)
    start_z(1)
    start_x(1)
    ring_middle(*ring_x, k_x[0], cut_x[0])
    ring_middle(*ring_x, k_x[1], cut_x[1])
    ring_middle(*ring_z, k_z[0], CUTS[0])
    give_back(0)
    ring_middle(*ring_z, k_z[1], CUTS[1])
    give_back(1)
    for q in range(2):
        arrive(returned.at[halves[q]], k_back[q])
    spaced = dot(pick[...], returned[...], (1, 0)).reshape(STRIPS, TILE, CH)
    grad_input[...] = spaced[:, 0:7, :].astype(BF16)
    for j in range(2):
        grad_weight[:, halves[j]] = ring_end(zb, z_left, z_right, k_z[j], CUTS[j]).T.astype(BF16)
    for copy in started:
        copy.wait_send()


def on_device(activations, conv_weight, norm_gain, norm_bias, cotangent):
    images = activations.shape[1]
    acts = activations.reshape(images, 7, 2, 14, CH)
    cotan = cotangent.reshape(images, 7, 7, COLS)
    hbm = pl.BlockSpec(memory_space=pltpu.HBM)
    results = (
        jax.ShapeDtypeStruct((STRIPS, 7, COLS), BF16),
        jax.ShapeDtypeStruct((STRIPS, 7, CH), BF16),
        jax.ShapeDtypeStruct((COLS, COLS), BF16),
        jax.ShapeDtypeStruct((2, COLS), F32),
    )
    block_out, grad_input, grad_weight, grads = pl.pallas_call(
        kernel,
        out_shape=results,
        in_specs=[hbm] * 5,
        out_specs=[pl.BlockSpec(memory_space=pltpu.VMEM)] * 4,
        scratch_shapes=[
            pltpu.VMEM((images, 7, 14, CH), BF16),
            pltpu.VMEM((STRIPS, TILE, CH), BF16),
            pltpu.VMEM((RING * 2 * CH, COLS), BF16),
            pltpu.VMEM((1, COLS), F32),
            pltpu.VMEM((1, COLS), F32),
            pltpu.VMEM((images, 7, 7, COLS), BF16),
            pltpu.VMEM((STRIPS, TILE, COLS), BF16),
            pltpu.VMEM((STRIPS * TILE, PAD), BF16),
            pltpu.VMEM((PAD, CH), BF16),
            pltpu.VMEM((RING, 2, PAD, CH), BF16),
            pltpu.VMEM((RING, RING, 2, HALF, COLS), BF16),
            pltpu.VMEM((RING, PAD, COLS), BF16),
            pltpu.VMEM((PAD, COLS), BF16),
            pltpu.VMEM((COLS, RING * PAD), BF16),
            pltpu.VMEM((PAD, COLS), F32),
            pltpu.VMEM((PAD, COLS), F32),
            pltpu.VMEM((PAD, COLS), BF16),
            pltpu.VMEM((RING * RING, 2, COLS), F32),
            pltpu.VMEM((RING * RING, 2, COLS), F32),
            pltpu.VMEM((RING, CH, COLS), BF16),
            pltpu.VMEM((PAD, COLS), BF16),
            pltpu.VMEM((RING, PAD, CH), BF16),
            pltpu.VMEM((PAD, CH), BF16),
            pltpu.VMEM((PAD, CH), BF16),
            pltpu.VMEM((PAD, CH), BF16),
            pltpu.VMEM((RING, COLS, COLS), BF16),
            pltpu.VMEM((COLS, COLS), BF16),
            pltpu.VMEM((COLS, COLS), BF16),
            pltpu.VMEM((COLS, COLS), BF16),
            pltpu.VMEM((PAD, CH), BF16),
            pltpu.VMEM((PAD, CH), BF16),
            pltpu.SemaphoreType.DMA((COPIES,)),
            pltpu.SemaphoreType.DMA((COPIES,)),
            pltpu.SemaphoreType.DMA((7,)),
            pltpu.SemaphoreType.REGULAR,
        ],
        compiler_params=pltpu.CompilerParams(
            collective_id=0, has_side_effects=True, vmem_limit_bytes=VMEM_BYTES
        ),
        name="bottleneck",
    )(*(pltpu.with_memory_space_constraint(a, pltpu.HBM) for a in (acts, conv_weight[0], norm_gain, norm_bias, cotan)))
    return (
        block_out.reshape(1, images, 7, 7, COLS),
        grad_input.reshape(1, images, 7, 7, CH),
        grad_weight[None],
        grads[1:2],
        grads[0:1],
    )


def solution(mesh):
    placed = (
        P("section", "dp", None, None, "mp"),
        P("section", None, "mp"),
        P("section", "mp"),
        P("section", "mp"),
        P("section", "dp", None, None, "mp"),
    )
    return jax.shard_map(
        on_device,
        mesh=mesh,
        in_specs=placed,
        out_specs=(
            P("section", "dp", None, None, "mp"),
            P("section", "dp", None, None, "mp"),
            P("section", "dp", "mp"),
            P("section", "mp"),
            P("section", "mp"),
        ),
        check_vma=False,
    )
```

```python
import functools

import jax
import jax.numpy as jnp
from jax import lax
from jax.experimental import pallas as pl
from jax.experimental.pallas import tpu as pltpu
from jax.sharding import PartitionSpec as P

BF16 = jnp.bfloat16
F32 = jnp.float32
RING = 4
ROWS = 245
PAD = 256
HALF = PAD // 2
CH = 512
COLS = 256
TILE = 16
STRIPS = 35
COPIES = 192
FAR_FIRST = (8, 7, 9, 6, 10, 5, 11, 4, 12, 3, 13, 2, 14, 1, 15)
BAND = 64
CUTS = ((0, 128), (128, 256))
PARTS = 8
VMEM_BYTES = 40 * 2**20


def dot(a, b, over):
    return lax.dot_general(a, b, ((over[:1], over[1:]), ((), ())), preferred_element_type=F32)


def picks(step, back=False, rows=(0, PAD), strips=(0, STRIPS)):
    shape = (rows[1] - rows[0], (strips[1] - strips[0]) * TILE)
    shape = shape[::-1] if back else shape
    row = rows[0] + lax.broadcasted_iota(jnp.int32, shape, 1 if back else 0)
    col = strips[0] * TILE + lax.broadcasted_iota(jnp.int32, shape, 0 if back else 1)
    pixel = col & (TILE - 1)
    wanted = 7 * (col >> 4) + (pixel if step == 1 else pixel >> 1)
    keep = (row == wanted) & (pixel < 7 * step)
    if step == 2:
        keep = keep & ((pixel & 1) == 0)
    return jnp.where(keep, 1.0, 0.0).astype(F32).astype(BF16)


def kernel(
    acts, weight, gain_hbm, shift_hbm, cotan,
    block_out, grad_input, grad_weight, grads,
    raw, strips, w, gain_ref, shift_ref, ct_raw, ct_strips, pick, own, full, ex, own_rows, mine, across, hid, cot, acted,
    stat, grad,
    w_mate, mate, xb, x_opp, x_left, x_right,
    zb, z_opp, z_left, z_right, share, returned,
    send_sems, recv_sems, local_sems, met_sem,
):
    section, dp, mp = lax.axis_index("section"), lax.axis_index("dp"), lax.axis_index("mp")
    zh, y = lax.div(dp, RING), lax.rem(dp, RING)
    x, core = lax.div(mp, 2), lax.rem(mp, 2)

    def around(at, by):
        return lax.rem(at + by, RING)

    partner = {"section": section + 1 - 2 * lax.rem(section, 2)}
    sibling = {"mp": 2 * x + 1 - core}
    at_x = [{"mp": 2 * around(x, o) + core} for o in range(RING)]
    at_y = [{"dp": RING * zh + around(y, o)} for o in range(RING)]
    at_z = [{"dp": RING * around(zh, o) + y} for o in range(RING)]
    others = [{"dp": lax.rem(dp + o, RING * RING)} for o in FAR_FIRST]
    near = [partner, at_x[1], at_x[3]] + at_y[1:]
    far = [{"dp": RING * around(zh, i) + around(y, j)} for i in (2, 1, 3) for j in range(RING)]

    started = []
    ids = iter(range(COPIES))

    def names(n):
        return [next(ids) for _ in range(n)]

    def send(src, dst, k, to):
        copy = pltpu.make_async_remote_copy(
            src_ref=src, dst_ref=dst, send_sem=send_sems.at[k], recv_sem=recv_sems.at[k],
            device_id=to, device_id_type=pl.DeviceIdType.MESH,
        )
        copy.start()
        started.append(copy)

    def arrive(dst, k):
        pltpu.make_async_remote_copy(
            src_ref=dst, dst_ref=dst, send_sem=send_sems.at[k], recv_sem=recv_sems.at[k],
            device_id=sibling, device_id_type=pl.DeviceIdType.MESH,
        ).wait_recv()

    early = 2
    load_first = pltpu.make_async_copy(acts.at[0:early, :, 0], raw.at[0:early], local_sems.at[0])
    load_rest = pltpu.make_async_copy(acts.at[early:, :, 0], raw.at[early:], local_sems.at[6])
    load_w = pltpu.make_async_copy(weight, w, local_sems.at[1])
    load_ct = pltpu.make_async_copy(cotan, ct_raw, local_sems.at[2])
    load_gain = pltpu.make_async_copy(gain_hbm, gain_ref, local_sems.at[4])
    load_shift = pltpu.make_async_copy(shift_hbm, shift_ref, local_sems.at[5])
    load_first.start()
    load_rest.start()
    load_ct.start()
    load_w.start()
    load_gain.start()
    load_shift.start()
    barrier = pltpu.get_barrier_semaphore()

    def signal(sem, to):
        pl.semaphore_signal(sem, inc=1, device_id=to, device_id_type=pl.DeviceIdType.MESH)

    @pl.when(core == 1)
    def _():
        signal(barrier, sibling)

    for to in near:
        signal(barrier, {"mp": 2 * x, **to, **({"mp": to["mp"] - core} if "mp" in to else {})})
    for to in far:
        signal(barrier, {"mp": 2 * x + 1, **to})
    strips[:, 14:TILE, :] = jnp.zeros((STRIPS, TILE - 14, CH), BF16)
    size = PAD // PARTS
    parts = [pl.ds(p * size, size) for p in range(PARTS)]

    def sample(p):
        first, last = p * size // 7, min(((p + 1) * size - 1) // 7 + 1, STRIPS)
        choose = picks(2, rows=(p * size, (p + 1) * size), strips=(first, last))
        pixels = strips[first:last].reshape((last - first) * TILE, CH)
        own[parts[p], :] = dot(choose, pixels, (1, 0)).astype(BF16)

    load_first.wait()
    strips[0 : 7 * early, 0:14, :] = raw[0:early].reshape(7 * early, 14, CH)
    sample(0)
    @pl.when(core == 0)
    def _():
        pl.semaphore_wait(barrier, 2 * len(near) + 1)
        signal(met_sem, sibling)

    @pl.when(core == 1)
    def _():
        pl.semaphore_wait(met_sem, 1)


    k_part, k_left, k_right, k_sib = names(PARTS), names(PARTS), names(PARTS), names(PARTS)
    k_sl, k_sr, k_so, k_opp = names(PARTS), names(PARTS), names(PARTS), names(PARTS)
    for p in range(PARTS):
        if p == 1:
            load_rest.wait()
            strips[7 * early :, 0:14, :] = raw[early:].reshape(STRIPS - 7 * early, 14, CH)
        if p > 0:
            sample(p)
        send(own.at[parts[p]], full.at[x, core, parts[p]], k_part[p], partner)
    ct_strips[...] = jnp.zeros_like(ct_strips)
    for p in range(PARTS):
        here = full.at[x, core, parts[p]]
        arrive(here, k_part[p])
        send(here, here, k_right[p], at_x[1])
        send(here, here, k_left[p], at_x[3])
        send(here, here, k_sib[p], sibling)
        if p == 0:
            load_ct.wait()
            ct_strips[:, 0:7, :] = ct_raw[...].reshape(STRIPS, 7, COLS)
            cot[...] = dot(picks(1), ct_strips[...].reshape(STRIPS * TILE, COLS), (1, 0))
            pick[...] = picks(1, back=True)
            load_w.wait()
            load_gain.wait()
            load_shift.wait()

    def w_block(xx, cc):
        return w[pl.ds(pl.multiple_of(CH * (2 * xx + cc), CH), CH), :]

    def term(xx, cc):
        return dot(full[xx, cc], w_block(xx, cc), (1, 0))

    k_ex, k_xl, k_xr, k_xo, k_es = names(RING), names(2), names(2), names(2), names(RING)

    def exchange():
        for o in (2, 1, 3):
            yy = around(y, o)
            at = pl.multiple_of(COLS * lax.rem(yy, 2), COLS)
            rows = pl.ds(pl.multiple_of(HALF * core, HALF), HALF)
            send(
                full.at[x, lax.div(yy, 2), rows, pl.ds(at, COLS)],
                ex.at[x, RING - o, core], k_ex[o], at_y[o],
            )

    def others_of(xx, cc, h=None):
        rows = pl.ds(0, HALF) if h is None else pl.ds(h * BAND, BAND)
        return ex.at[xx, pl.ds(1, RING - 1), cc, rows]

    def along_x():
        for o in range(1, RING):
            arrive(ex.at[x, RING - o, core], k_ex[o])
        for h in range(2):
            send(others_of(x, core, h), others_of(x, core, h), k_xl[h], at_x[1])
            send(others_of(x, core, 1 - h), others_of(x, core, 1 - h), k_xr[1 - h], at_x[3])
        send(others_of(x, core), others_of(x, core), k_es[0], sibling)

    def farther_x():
        arrive(others_of(lx, core, 0), k_xl[0])
        send(others_of(lx, core, 0), others_of(lx, core, 0), k_xo[0], at_x[1])
        arrive(others_of(rx, core, 1), k_xr[1])
        send(others_of(rx, core, 1), others_of(rx, core, 1), k_xo[1], at_x[3])
        arrive(others_of(lx, core, 1), k_xl[1])
        send(others_of(lx, core), others_of(lx, core), k_es[1], sibling)
        arrive(others_of(rx, core, 0), k_xr[0])
        send(others_of(rx, core), others_of(rx, core), k_es[2], sibling)

    def last_x():
        arrive(others_of(ox, core, 0), k_xo[0])
        arrive(others_of(ox, core, 1), k_xo[1])
        send(others_of(ox, core), others_of(ox, core), k_es[3], sibling)

    lx, rx, ox = around(x, 3), around(x, 1), around(x, 2)
    for p in range(PARTS):
        from_left = full.at[lx, core, parts[p]]
        arrive(from_left, k_right[p])
        if p < PARTS // 2:
            send(from_left, from_left, k_opp[p], at_x[1])
        send(from_left, from_left, k_sl[p], sibling)
        from_right = full.at[rx, core, parts[p]]
        arrive(from_right, k_left[p])
        if p >= PARTS // 2:
            send(from_right, from_right, k_opp[p], at_x[3])
        send(from_right, from_right, k_sr[p], sibling)
        if p == 0:
            for q in range(PARTS):
                arrive(full.at[x, 1 - core, parts[q]], k_sib[q])
            exchange()
    hid[...] = term(x, core)
    hid[...] += term(x, 1 - core)
    hid[...] += term(lx, core)
    hid[...] += term(rx, core)
    for p in range(PARTS):
        arrive(full.at[lx, 1 - core, parts[p]], k_sl[p])
        arrive(full.at[rx, 1 - core, parts[p]], k_sr[p])
    hid[...] += term(lx, 1 - core)
    hid[...] += term(rx, 1 - core)
    for p in range(PARTS):
        opposite = full.at[ox, core, parts[p]]
        arrive(opposite, k_opp[p])
        send(opposite, opposite, k_so[p], sibling)
    hid[...] += term(ox, core)
    for p in range(PARTS):
        arrive(full.at[ox, 1 - core, parts[p]], k_so[p])
    hid[...] += term(ox, 1 - core)

    def tell(buf, a, b, ks):
        first = lax.broadcasted_iota(jnp.int32, (2, COLS), 0) == 0
        buf[dp] = jnp.where(first, a, b)
        for k, to in zip(ks, others):
            send(buf.at[dp], buf.at[dp], k, to)

    def hear(buf, ks):
        for k, o in zip(ks, FAR_FIRST):
            arrive(buf.at[lax.rem(dp + RING * RING - o, RING * RING)], k)
        return buf[...]

    bands = [pl.ds(b * BAND, BAND) for b in range(PAD // BAND)]
    mean = sum(jnp.sum(hid[band, :], axis=0, keepdims=True) for band in bands) / ROWS
    square = jnp.zeros_like(mean)
    for b, band in enumerate(bands):
        off = hid[band, :] - mean
        if (b + 1) * BAND > ROWS:
            row = lax.broadcasted_iota(jnp.int32, (BAND, COLS), 0)
            off = jnp.where(row < ROWS - b * BAND, off, 0.0)
        square += jnp.sum(off * off, axis=0, keepdims=True)
    k_stat, k_grad = names(15), names(15)
    @pl.when(core == 1)
    def _():
        pl.semaphore_wait(barrier, 2 * len(far))
        signal(met_sem, sibling)

    @pl.when(core == 0)
    def _():
        pl.semaphore_wait(met_sem, 1)

    tell(stat, mean, square, k_stat)
    along_x()
    k_w = names(RING)
    for xx in range(RING):
        send(w.at[pl.ds(pl.multiple_of(CH * (2 * xx + 1 - core), CH), CH), :], w_mate.at[xx], k_w[xx], sibling)
    keep = pltpu.make_async_copy(
        full.at[:, lax.div(y, 2), :, pl.ds(pl.multiple_of(COLS * lax.rem(y, 2), COLS), COLS)],
        own_rows, local_sems.at[3],
    )
    keep.start()

    heard = hear(stat, k_stat)
    means = heard[:, 0:1, :]
    mean = jnp.sum(means, axis=0) / (RING * RING)
    square = jnp.sum(heard[:, 1:2, :] + ROWS * (means - mean) * (means - mean), axis=0)
    total = float(ROWS * RING * RING)
    inverse = lax.rsqrt(square / total + 1e-05)
    gain, shift = gain_ref[...], shift_ref[...]
    d_bias, d_gain = jnp.zeros_like(mean), jnp.zeros_like(mean)
    for band in bands:
        normed = (hid[band, :] - mean) * inverse
        pre_act = gain * normed + shift
        squash = 0.5 * jnp.tanh(0.5 * pre_act) + 0.5
        acted[band, :] = (pre_act * squash).astype(BF16)
        grad_pre = cot[band, :] * (squash * (1.0 + pre_act * (1.0 - squash)))
        cot[band, :] = grad_pre
        d_bias += jnp.sum(grad_pre, axis=0, keepdims=True)
        d_gain += jnp.sum(grad_pre * normed, axis=0, keepdims=True)
    tell(grad, d_bias, d_gain, k_grad)

    farther_x()
    sums = jnp.sum(hear(grad, k_grad), axis=0)
    d_bias, d_gain = sums[0:1, :], sums[1:2, :]
    scale = gain * inverse
    less, tilt = d_bias / total, inverse * (d_gain / total)
    for band in bands:
        part = scale * (cot[band, :] - less - (hid[band, :] - mean) * tilt)
        mine[band, :] = part.astype(BF16)

    halves = [pl.ds(0, HALF), pl.ds(HALF, HALF)]

    k_y = [names(RING) for _ in CUTS]
    order = (2, 1, 3, 0)

    def across_from(j, r):
        return across.at[pl.ds(CUTS[j][0], CUTS[j][1] - CUTS[j][0]), pl.ds(PAD * r, PAD)]

    k_mate = names(2)
    for q in range(2):
        send(mine.at[halves[q]], mate.at[halves[q]], k_mate[q], sibling)
    across[:, 0:PAD] = mine[...].T
    for j in range(len(CUTS)):
        for o in (2, 1, 3):
            send(across_from(j, 0), across_from(j, RING - o), k_y[j][o], at_y[o])

    last_x()

    def ring_start(block, opp, left, right, to, ks, cut, make):
        lo, hi = pl.ds(cut[0], (cut[1] - cut[0]) // 2), pl.ds((cut[0] + cut[1]) // 2, (cut[1] - cut[0]) // 2)
        make(2)
        send(block.at[2, lo], opp.at[lo], ks[0], to[1])
        send(block.at[2, hi], opp.at[hi], ks[1], to[3])
        make(1)
        send(block.at[1, hi], left.at[hi], ks[2], to[1])
        make(3)
        send(block.at[3, lo], right.at[lo], ks[3], to[3])
        make(0)

    def ring_middle(block, opp, left, right, to, ks, cut):
        lo, hi = pl.ds(cut[0], (cut[1] - cut[0]) // 2), pl.ds((cut[0] + cut[1]) // 2, (cut[1] - cut[0]) // 2)
        arrive(opp.at[lo], ks[0])
        block[1, lo] = (block[1, lo].astype(F32) + opp[lo].astype(F32)).astype(BF16)
        send(block.at[1, lo], left.at[lo], ks[4], to[1])
        arrive(opp.at[hi], ks[1])
        block[3, hi] = (block[3, hi].astype(F32) + opp[hi].astype(F32)).astype(BF16)
        send(block.at[3, hi], right.at[hi], ks[5], to[3])

    def ring_end(block, left, right, ks, cut):
        lo, hi = pl.ds(cut[0], (cut[1] - cut[0]) // 2), pl.ds((cut[0] + cut[1]) // 2, (cut[1] - cut[0]) // 2)
        arrive(left.at[hi], ks[2])
        arrive(right.at[lo], ks[3])
        arrive(left.at[lo], ks[4])
        arrive(right.at[hi], ks[5])
        rows = slice(*cut)
        return block[0, rows].astype(F32) + left[rows].astype(F32) + right[rows].astype(F32)

    k_x, k_z, k_back = [names(6), names(6)], [names(6) for _ in CUTS], names(2)
    ring_x = (xb, x_opp, x_left, x_right, at_x)
    ring_z = (zb, z_opp, z_left, z_right, at_z)
    cut_x = ((0, HALF), (HALF, PAD))

    def start_x(q):
        def make(o):
            part = dot(mine[halves[q], :], w_block(around(x, o), core), (1, 1))
            part += dot(mate[halves[q], :], w_mate[around(x, o)], (1, 1))
            xb[o, halves[q]] = part.astype(BF16)

        arrive(mate.at[halves[q]], k_mate[q])
        ring_start(*ring_x, k_x[q], cut_x[q], make)

    def start_z(j):
        for o in range(1, RING):
            arrive(across_from(j, RING - o), k_y[j][o])
        rows = slice(*CUTS[j])

        def make(o):
            slot = around(zh, o)
            rest = ex[slot, 1:RING].reshape((RING - 1) * PAD, COLS)
            block = dot(across[rows, 0:PAD], own_rows[slot], (1, 0))
            zb[o, rows] = (block + dot(across[rows, PAD:], rest, (1, 0))).astype(BF16)

        ring_start(*ring_z, k_z[j], CUTS[j], make)

    def give_back(q):
        share[halves[q], :] = ring_end(xb, x_left, x_right, k_x[q], cut_x[q]).astype(BF16)
        send(share.at[halves[q]], returned.at[halves[q]], k_back[q], partner)

    for xx in range(RING):
        arrive(w_mate.at[xx], k_w[xx])
    start_x(0)
    spaced = dot(pick[...], acted[...], (1, 0)).reshape(STRIPS, TILE, COLS)
    block_out[...] = spaced[:, 0:7, :].astype(BF16)
    grads[...] = sums

    keep.wait()
    for i, xx in enumerate((x, lx, rx, ox)):
        arrive(others_of(xx, 1 - core), k_es[i])
    start_z(0)
    start_z(1)
    start_x(1)
    ring_middle(*ring_x, k_x[0], cut_x[0])
    ring_middle(*ring_x, k_x[1], cut_x[1])
    ring_middle(*ring_z, k_z[0], CUTS[0])
    give_back(0)
    ring_middle(*ring_z, k_z[1], CUTS[1])
    give_back(1)
    for q in range(2):
        arrive(returned.at[halves[q]], k_back[q])
    spaced = dot(pick[...], returned[...], (1, 0)).reshape(STRIPS, TILE, CH)
    grad_input[...] = spaced[:, 0:7, :].astype(BF16)
    for j in range(2):
        grad_weight[:, halves[j]] = ring_end(zb, z_left, z_right, k_z[j], CUTS[j]).T.astype(BF16)
    for copy in started:
        copy.wait_send()


def on_device(activations, conv_weight, norm_gain, norm_bias, cotangent):
    images = activations.shape[1]
    acts = activations.reshape(images, 7, 2, 14, CH)
    cotan = cotangent.reshape(images, 7, 7, COLS)
    hbm = pl.BlockSpec(memory_space=pltpu.HBM)
    results = (
        jax.ShapeDtypeStruct((STRIPS, 7, COLS), BF16),
        jax.ShapeDtypeStruct((STRIPS, 7, CH), BF16),
        jax.ShapeDtypeStruct((COLS, COLS), BF16),
        jax.ShapeDtypeStruct((2, COLS), F32),
    )
    block_out, grad_input, grad_weight, grads = pl.pallas_call(
        kernel,
        out_shape=results,
        in_specs=[hbm] * 5,
        out_specs=[pl.BlockSpec(memory_space=pltpu.VMEM)] * 4,
        scratch_shapes=[
            pltpu.VMEM((images, 7, 14, CH), BF16),
            pltpu.VMEM((STRIPS, TILE, CH), BF16),
            pltpu.VMEM((RING * 2 * CH, COLS), BF16),
            pltpu.VMEM((1, COLS), F32),
            pltpu.VMEM((1, COLS), F32),
            pltpu.VMEM((images, 7, 7, COLS), BF16),
            pltpu.VMEM((STRIPS, TILE, COLS), BF16),
            pltpu.VMEM((STRIPS * TILE, PAD), BF16),
            pltpu.VMEM((PAD, CH), BF16),
            pltpu.VMEM((RING, 2, PAD, CH), BF16),
            pltpu.VMEM((RING, RING, 2, HALF, COLS), BF16),
            pltpu.VMEM((RING, PAD, COLS), BF16),
            pltpu.VMEM((PAD, COLS), BF16),
            pltpu.VMEM((COLS, RING * PAD), BF16),
            pltpu.VMEM((PAD, COLS), F32),
            pltpu.VMEM((PAD, COLS), F32),
            pltpu.VMEM((PAD, COLS), BF16),
            pltpu.VMEM((RING * RING, 2, COLS), F32),
            pltpu.VMEM((RING * RING, 2, COLS), F32),
            pltpu.VMEM((RING, CH, COLS), BF16),
            pltpu.VMEM((PAD, COLS), BF16),
            pltpu.VMEM((RING, PAD, CH), BF16),
            pltpu.VMEM((PAD, CH), BF16),
            pltpu.VMEM((PAD, CH), BF16),
            pltpu.VMEM((PAD, CH), BF16),
            pltpu.VMEM((RING, COLS, COLS), BF16),
            pltpu.VMEM((COLS, COLS), BF16),
            pltpu.VMEM((COLS, COLS), BF16),
            pltpu.VMEM((COLS, COLS), BF16),
            pltpu.VMEM((PAD, CH), BF16),
            pltpu.VMEM((PAD, CH), BF16),
            pltpu.SemaphoreType.DMA((COPIES,)),
            pltpu.SemaphoreType.DMA((COPIES,)),
            pltpu.SemaphoreType.DMA((7,)),
            pltpu.SemaphoreType.REGULAR,
        ],
        compiler_params=pltpu.CompilerParams(
            collective_id=0, has_side_effects=True, vmem_limit_bytes=VMEM_BYTES
        ),
        name="bottleneck",
    )(*(pltpu.with_memory_space_constraint(a, pltpu.HBM) for a in (acts, conv_weight[0], norm_gain, norm_bias, cotan)))
    return (
        block_out.reshape(1, images, 7, 7, COLS),
        grad_input.reshape(1, images, 7, 7, CH),
        grad_weight[None],
        grads[1:2],
        grads[0:1],
    )


def solution(mesh):
    placed = (
        P("section", "dp", None, None, "mp"),
        P("section", None, "mp"),
        P("section", "mp"),
        P("section", "mp"),
        P("section", "dp", None, None, "mp"),
    )
    return jax.shard_map(
        on_device,
        mesh=mesh,
        in_specs=placed,
        out_specs=(
            P("section", "dp", None, None, "mp"),
            P("section", "dp", None, None, "mp"),
            P("section", "dp", "mp"),
            P("section", "mp"),
            P("section", "mp"),
        ),
        check_vma=False,
    )
```
